32 devices in a mesh: walk: 16 (over z, y, x), col: 2 (over core).
Axes of the slice: x: 2, y: 2, z: 4, core: 2. Of those that a mesh axis runs over, the one named last changes fastest.
Arguments:
- jacobian: float32 [96, 32768], P('walk', 'col'), may hold values from -25 to 25
- prev_update: float32 [2, 16384], P('col', 'walk'), may hold values from -6 to 6
- base_energy: float32 [96], P('walk'), may hold values from -6 to 6
- elec_pos: float32 [96, 3, 66], P('walk'), may hold values from -8 to 8
- atom_pos: float32 [3, 21], replicated, may hold values from -6 to 6
- quad_ratio: float32 [96, 21, 66, 12], P('walk'), may hold values from -1.2 to 1.2
- rotation: int32 [96, 66], P('walk'), may hold values from 0 to 15
- channels: int32 [21], replicated, may hold values from 1 to 3
- ecp_coef: float32 [21, 3], replicated, may hold values from 0.5 to 2
- ecp_expo: float32 [21, 3], replicated, may hold values from 0.2 to 2
Outputs:
- local_energy: float32 [96], P('walk')
- update: float32 [2, 16384], P('col', 'walk')
The draws below stay inside these ranges and needn't reach their ends.
All inputs are finite; a program needn't handle non-finite values.
Results may differ from the reference program's by a relative error of at most 0.0003.
Values sent between devices are 32-bit elements; how exact they have to be, the bound alone decides.
A program may use at most 64 MiB of HBM per device.

```python
import math
import jax
import jax.numpy as jnp
from jax import lax

NE = 66
NA = 21
QUAD = 12
LMAX = 3
NROT = 16
WALKERS = 96
PARAMS = 32768
N_COL = 2


def draw_jacobian(key, part):
    keys = jax.random.split(key, 4)
    noise = jnp.clip(jax.random.normal(keys[0], (WALKERS, PARAMS), jnp.float32), -5.0, 5.0)
    spread = jnp.exp(jax.random.uniform(keys[1], (WALKERS,), jnp.float32) * math.log(3.0))
    row_factor = jnp.clip(jax.random.normal(keys[2], (4, WALKERS), jnp.float32), -4.0, 4.0)
    col_factor = jnp.clip(0.06 * jax.random.normal(keys[3], (4, PARAMS), jnp.float32), -0.3, 0.3)
    total = spread[:, None] * noise
    for index in range(4):
        total = total + row_factor[index][:, None] * col_factor[index][None, :]
    return total


def place_ends(entries, key, smallest, top_value):
    extent = entries.shape
    index_at = [jax.random.randint(jax.random.fold_in(key, axis), (), 0, extent[axis]) for axis in range(len(extent))]
    entries = entries.at[tuple(index_at)].set(smallest)
    longest = extent.index(max(extent))
    index_at[longest] = (index_at[longest] + 1) % extent[longest]
    return entries.at[tuple(index_at)].set(top_value)


def steps_of(own_key, dims, shards, smallest, largest):
    level = 1.0
    for position, blocks in shards:
        draws = jax.random.uniform(jax.random.fold_in(jax.random.fold_in(own_key, 6), position), (blocks,), jnp.float32, smallest / len(shards), largest / len(shards))
        level = level * jnp.repeat(jnp.exp(draws), dims[position] // blocks).reshape((-1,) + (1,) * (len(dims) - 1 - position))
    return level


def bell_draw(stream_key, dims, scale, bound, cuts=(), kind=jnp.bfloat16):
    drawn = jax.random.normal(stream_key, dims, jnp.float32) * scale
    if len(cuts) > 0:
        drawn = steps_of(stream_key, dims, cuts, -0.22, 0.18) * drawn
    return jnp.clip(drawn, min=-bound, max=bound).astype(kind)


def setup_inputs(seed: int = 0) -> dict:
    key_list = jax.random.split(jax.random.key(seed), 11)
    jacobian = draw_jacobian(jax.random.fold_in(key_list[10], 71), 0)
    prev_update = bell_draw(key_list[1], (N_COL, PARAMS // N_COL), 1.0, 6.0, ((0, 2), (1, 16)), jnp.float32)
    base_energy = bell_draw(key_list[2], (WALKERS,), 1.0, 6.0, ((0, 16),), jnp.float32)
    elec_pos = bell_draw(key_list[3], (WALKERS, 3, NE), 1.5, 8.0, ((0, 16),), jnp.float32)
    atom_pos = bell_draw(key_list[4], (3, NA), 1.5, 6.0, (), jnp.float32)
    quad_ratio = bell_draw(key_list[5], (WALKERS, NA, NE, QUAD), 0.2, 1.2, ((0, 16),), jnp.float32)
    rotation = place_ends(jax.random.randint(key_list[6], (WALKERS, NE), 0, NROT), jax.random.fold_in(key_list[6], 1), 0, NROT - 1).astype(jnp.int32)
    channels = place_ends(jax.random.randint(key_list[7], (NA,), 1, LMAX + 1), jax.random.fold_in(key_list[7], 1), 1, LMAX).astype(jnp.int32)
    ecp_coef = jnp.clip(jax.random.uniform(key_list[8], (NA, LMAX), jnp.float32, 0.5, 2.0), 0.5, 2.0)
    ecp_expo = jnp.clip(jnp.exp(jax.random.uniform(key_list[9], (NA, LMAX), jnp.float32, math.log(0.2), math.log(2.0))), 0.2, 2.0)
    return dict(jacobian=jacobian, prev_update=prev_update, base_energy=base_energy, elec_pos=elec_pos, atom_pos=atom_pos, quad_ratio=quad_ratio, rotation=rotation, channels=channels, ecp_coef=ecp_coef, ecp_expo=ecp_expo)


momentum = 0.9
damping = 0.1

def icosa_points():
    golden = (1.0 + math.sqrt(5.0)) / 2.0
    length = math.sqrt(1.0 + golden * golden)
    rows = []
    for first in (-1.0, 1.0):
        for second in (-golden, golden):
            rows.append((0.0, first / length, second / length))
            rows.append((first / length, second / length, 0.0))
            rows.append((second / length, 0.0, first / length))
    return jnp.asarray(rows, dtype=jnp.float32).T

def rotation_table(count):
    angle = jnp.arange(count, dtype=jnp.float32)
    turn_z = 2.0 * math.pi * angle / count
    turn_x = 0.9 * angle
    cz, sz = (jnp.cos(turn_z), jnp.sin(turn_z))
    cx, sx = (jnp.cos(turn_x), jnp.sin(turn_x))
    zeros = jnp.zeros_like(cz)
    matrix = jnp.stack([jnp.stack([cz, -sz * cx, sz * sx], axis=-1), jnp.stack([sz, cz * cx, -cz * sx], axis=-1), jnp.stack([zeros, sx, cx], axis=-1)], axis=1)
    points = icosa_points()
    rotated = matrix[:, :, 0, None] * points[None, 0, :]
    rotated = rotated + matrix[:, :, 1, None] * points[None, 1, :]
    rotated = rotated + matrix[:, :, 2, None] * points[None, 2, :]
    return rotated.reshape(count, -1)

def nonlocal_energy(elec_pos, atom_pos, quad_ratio, rotation, channels, ecp_coef, ecp_expo):
    walkers, electrons = rotation.shape
    count = NROT
    table = rotation_table(count)
    onehot = (rotation[:, :, None] == jnp.arange(count, dtype=jnp.int32)[None, None, :]).astype(jnp.float32)
    rotated = jnp.einsum('wek,kf->wef', onehot, table, precision=lax.Precision.HIGHEST)
    rotated = rotated.reshape(walkers, electrons, 3, -1)
    diff = elec_pos[:, :, None, :] - atom_pos[None, :, :, None]
    dist2 = lax.optimization_barrier(jnp.sum(diff * diff, axis=1))
    unit = diff / jnp.sqrt(dist2 + 0.01)[:, None, :, :]
    cosang = unit[:, 0, :, :, None] * rotated[:, None, :, 0, :]
    cosang = cosang + unit[:, 1, :, :, None] * rotated[:, None, :, 1, :]
    cosang = cosang + unit[:, 2, :, :, None] * rotated[:, None, :, 2, :]
    quad = quad_ratio.shape[-1]
    lmax = ecp_coef.shape[1]
    lower = jnp.ones_like(cosang)
    upper = cosang
    total = jnp.zeros((walkers,), jnp.float32)
    for level in range(lmax):
        if level == 0:
            poly = lower
        elif level == 1:
            poly = upper
        else:
            fresh = ((2 * level - 1) * cosang * upper - (level - 1) * lower) / level
            lower, upper = (upper, fresh)
            poly = fresh
        angular = lax.optimization_barrier(jnp.sum(poly * quad_ratio, axis=-1)) / quad
        active = (channels > level).astype(jnp.float32)
        radial = ecp_coef[None, :, level, None] * jnp.exp(-ecp_expo[None, :, level, None] * dist2)
        term = (2 * level + 1) * active[None, :, None] * radial * angular
        total = total + lax.optimization_barrier(jnp.sum(term, axis=(1, 2)))
    return total

def reference(jacobian, prev_update, base_energy, elec_pos, atom_pos, quad_ratio, rotation, channels, ecp_coef, ecp_expo):
    local_energy = base_energy + nonlocal_energy(elec_pos, atom_pos, quad_ratio, rotation, channels, ecp_coef, ecp_expo)
    walkers, total = jacobian.shape
    width = math.gcd(total, 8192)
    count = total // width
    means = lax.optimization_barrier(jnp.mean(jacobian, axis=0))
    prev = prev_update.reshape(total)
    scale = 1.0 / total

    def accumulate(index, carry):
        gram, along = carry
        start = (index * width).astype(jnp.int32)
        block = lax.dynamic_slice_in_dim(jacobian, start, width, 1) - lax.dynamic_slice_in_dim(means, start, width, 0)[None, :]
        piece = lax.dynamic_slice_in_dim(prev, start, width, 0)
        gram = gram + jnp.dot(block.astype(jnp.float32), block.T.astype(jnp.float32), precision=lax.Precision.HIGHEST, preferred_element_type=jnp.float32) * scale
        along = along + jnp.dot(block.astype(jnp.float32), piece.astype(jnp.float32), precision=lax.Precision.HIGHEST, preferred_element_type=jnp.float32) * scale
        return (gram, along)
    gram, along = lax.fori_loop(0, count, accumulate, (jnp.zeros((walkers, walkers), jnp.float32), jnp.zeros((walkers,), jnp.float32)))
    eps = -(local_energy - jnp.mean(local_energy)) / math.sqrt(walkers)
    system = gram + damping * jnp.eye(walkers, dtype=jnp.float32)
    factor = jnp.linalg.cholesky(system)
    solved = jax.scipy.linalg.cho_solve((factor, True), eps - momentum * along)

    def project(index):
        start = (index * width).astype(jnp.int32)
        block = lax.dynamic_slice_in_dim(jacobian, start, width, 1) - lax.dynamic_slice_in_dim(means, start, width, 0)[None, :]
        piece = lax.dynamic_slice_in_dim(prev, start, width, 0)
        return jnp.dot(solved.astype(jnp.float32), block.astype(jnp.float32), precision=lax.Precision.HIGHEST, preferred_element_type=jnp.float32) + momentum * piece
    update = lax.map(project, jnp.arange(count, dtype=jnp.int32)).reshape(prev_update.shape)
    return (local_energy, update)
```

```python
import functools
import math

import jax
import jax.numpy as jnp
from jax import lax
from jax.experimental import pallas as pl
from jax.experimental.pallas import tpu as pltpu
from jax.sharding import PartitionSpec as P

NROT = 16


momentum = 0.9
damping = 0.1


def icosa_points():
    golden = (1.0 + math.sqrt(5.0)) / 2.0
    length = math.sqrt(1.0 + golden * golden)
    rows = []
    for first in (-1.0, 1.0):
        for second in (-golden, golden):
            rows.append((0.0, first / length, second / length))
            rows.append((first / length, second / length, 0.0))
            rows.append((second / length, 0.0, first / length))
    return jnp.asarray(rows, dtype=jnp.float32).T


def rotation_table(count):
    angle = jnp.arange(count, dtype=jnp.float32)
    turn_z = 2.0 * math.pi * angle / count
    turn_x = 0.9 * angle
    cz, sz = (jnp.cos(turn_z), jnp.sin(turn_z))
    cx, sx = (jnp.cos(turn_x), jnp.sin(turn_x))
    zeros = jnp.zeros_like(cz)
    matrix = jnp.stack(
        [
            jnp.stack([cz, -sz * cx, sz * sx], axis=-1),
            jnp.stack([sz, cz * cx, -cz * sx], axis=-1),
            jnp.stack([zeros, sx, cx], axis=-1),
        ],
        axis=1,
    )
    points = icosa_points()
    rotated = matrix[:, :, 0, None] * points[None, 0, :]
    rotated = rotated + matrix[:, :, 1, None] * points[None, 1, :]
    rotated = rotated + matrix[:, :, 2, None] * points[None, 2, :]
    return rotated.reshape(count, -1)


def nonlocal_energy(elec_pos, atom_pos, quad_ratio, rotation, channels, ecp_coef, ecp_expo):
    walkers, electrons = rotation.shape
    count = NROT
    table = rotation_table(count)
    onehot = (rotation[:, :, None] == jnp.arange(count, dtype=jnp.int32)[None, None, :]).astype(
        jnp.float32
    )
    rotated = jnp.einsum("wek,kf->wef", onehot, table, precision=lax.Precision.HIGHEST)
    rotated = rotated.reshape(walkers, electrons, 3, -1)
    diff = elec_pos[:, :, None, :] - atom_pos[None, :, :, None]
    dist2 = jnp.sum(diff * diff, axis=1)
    unit = diff / jnp.sqrt(dist2 + 0.01)[:, None, :, :]
    cosang = unit[:, 0, :, :, None] * rotated[:, None, :, 0, :]
    cosang = cosang + unit[:, 1, :, :, None] * rotated[:, None, :, 1, :]
    cosang = cosang + unit[:, 2, :, :, None] * rotated[:, None, :, 2, :]
    quad = quad_ratio.shape[-1]
    lmax = ecp_coef.shape[1]
    lower = jnp.ones_like(cosang)
    upper = cosang
    total = jnp.zeros((walkers,), jnp.float32)
    for level in range(lmax):
        if level == 0:
            poly = lower
        elif level == 1:
            poly = upper
        else:
            fresh = ((2 * level - 1) * cosang * upper - (level - 1) * lower) / level
            lower, upper = (upper, fresh)
            poly = fresh
        angular = jnp.sum(poly * quad_ratio, axis=-1) / quad
        active = (channels > level).astype(jnp.float32)
        radial = ecp_coef[None, :, level, None] * jnp.exp(-ecp_expo[None, :, level, None] * dist2)
        term = (2 * level + 1) * active[None, :, None] * radial * angular
        total = total + jnp.sum(term, axis=(1, 2))
    return total


MESH = pl.DeviceIdType.MESH
PAD = 8


def exchange_kernel(
    n,
    m,
    jac_ref,
    prev_ref,
    energy_ref,
    gram_ref,
    cent_ref,
    eall_ref,
    cols,
    part,
    shares,
    pair,
    full,
    ebuf,
    jac_send,
    jac_recv,
    e_send,
    e_recv,
    rs_send,
    rs_recv,
    pair_send,
    pair_recv,
    ag_send,
    ag_recv,
):
    me = lax.axis_index("walk")
    my_col = lax.axis_index("col")
    rows, width = cols.shape[1:]
    walkers = rows * n
    barrier = pltpu.get_barrier_semaphore()

    def greet(s, _):
        pl.semaphore_signal(
            barrier, inc=1, device_id=(lax.rem(me + s, n), my_col), device_id_type=MESH
        )
        return 0

    lax.fori_loop(1, n, greet, 0)
    for s in range(1, m):
        pl.semaphore_signal(
            barrier, inc=1, device_id=(me, lax.rem(my_col + s, m)), device_id_type=MESH
        )
    pl.semaphore_wait(barrier, n + m - 2)

    def block(index):
        return jac_ref.at[:, pl.ds(pl.multiple_of(index * width, width), width)]

    def jac_copy(s, origin):
        other = lax.rem(me + s, n)
        return pltpu.make_async_remote_copy(
            src_ref=block(other),
            dst_ref=cols.at[origin],
            send_sem=jac_send.at[s],
            recv_sem=jac_recv.at[origin],
            device_id=(other, my_col),
            device_id_type=MESH,
        )

    def tile_copy(src, dst, send, recv, s, origin):
        other = lax.rem(me + s, n)
        return pltpu.make_async_remote_copy(
            src_ref=src,
            dst_ref=dst.at[origin],
            send_sem=send.at[s],
            recv_sem=recv.at[origin],
            device_id=(other, my_col),
            device_id_type=MESH,
        )

    def start_jac(s, _):
        jac_copy(s, me).start()
        return 0

    lax.fori_loop(1, n, start_jac, 0)
    own = pltpu.make_async_copy(block(me), cols.at[me], jac_recv.at[me])
    own.start()

    ebuf[me] = energy_ref[...]

    def start_e(s, _):
        tile_copy(ebuf.at[me], ebuf, e_send, e_recv, s, me).start()
        return 0

    lax.fori_loop(1, n, start_e, 0)

    own.wait()

    def wait_jac(s, _):
        jac_copy(s, lax.rem(me + s, n)).wait_recv()
        return 0

    lax.fori_loop(1, n, wait_jac, 0)

    total = cols[0]
    for i in range(1, n):
        total = total + cols[i]
    mean = jnp.sum(total, axis=0, keepdims=True) * (1.0 / walkers)
    cent_ref[...] = jnp.zeros_like(cent_ref)
    for i in range(n):
        cent_ref[i, 0:rows, :] = cols[i] - mean
    cent_ref[0, rows : rows + 1, :] = prev_ref[...]
    cent = cent_ref[...].reshape(n * PAD, width)
    part[...] = lax.dot_general(
        cent,
        cent,
        (((1,), (1,)), ((), ())),
        precision=lax.Precision.HIGHEST,
        preferred_element_type=jnp.float32,
    ).reshape(part.shape)

    def start_rs(s, _):
        tile_copy(part.at[lax.rem(me + s, n)], shares, rs_send, rs_recv, s, me).start()
        return 0

    lax.fori_loop(1, n, start_rs, 0)
    shares[me] = part[me]

    def wait_rs(s, _):
        tile_copy(part.at[0], shares, rs_send, rs_recv, s, lax.rem(me + s, n)).wait_recv()
        return 0

    lax.fori_loop(1, n, wait_rs, 0)
    acc = shares[0]
    for i in range(1, n):
        acc = acc + shares[i]
    pair[my_col] = acc

    def pair_copy(s, origin):
        return pltpu.make_async_remote_copy(
            src_ref=pair.at[my_col],
            dst_ref=pair.at[origin],
            send_sem=pair_send.at[s],
            recv_sem=pair_recv.at[origin],
            device_id=(me, lax.rem(my_col + s, m)),
            device_id_type=MESH,
        )

    for s in range(1, m):
        pair_copy(s, my_col).start()
    for s in range(1, m):
        pair_copy(s, lax.rem(my_col + s, m)).wait_recv()
    acc = pair[0]
    for c in range(1, m):
        acc = acc + pair[c]
    full[me] = acc

    def start_ag(s, _):
        tile_copy(full.at[me], full, ag_send, ag_recv, s, me).start()
        return 0

    lax.fori_loop(1, n, start_ag, 0)

    def wait_e(s, _):
        tile_copy(ebuf.at[me], ebuf, e_send, e_recv, s, lax.rem(me + s, n)).wait_recv()
        return 0

    lax.fori_loop(1, n, wait_e, 0)
    eall_ref[...] = ebuf[...]

    def wait_ag(s, _):
        tile_copy(full.at[me], full, ag_send, ag_recv, s, lax.rem(me + s, n)).wait_recv()
        return 0

    lax.fori_loop(1, n, wait_ag, 0)
    gram_ref[...] = full[...]

    def wait_sends(s, _):
        jac_copy(s, me).wait_send()
        tile_copy(ebuf.at[me], ebuf, e_send, e_recv, s, me).wait_send()
        tile_copy(part.at[0], shares, rs_send, rs_recv, s, me).wait_send()
        tile_copy(full.at[me], full, ag_send, ag_recv, s, me).wait_send()
        return 0

    lax.fori_loop(1, n, wait_sends, 0)
    for s in range(1, m):
        pair_copy(s, my_col).wait_send()


def exchange(n, m, jacobian, prev_update, energy_tile):
    rows = jacobian.shape[0]
    width = jacobian.shape[1] // n
    wide = n * PAD
    vmem = pl.BlockSpec(memory_space=pltpu.VMEM)
    f32 = jnp.float32
    dma = pltpu.SemaphoreType.DMA
    return pl.pallas_call(
        functools.partial(exchange_kernel, n, m),
        out_shape=(
            jax.ShapeDtypeStruct((n, PAD, wide), f32),
            jax.ShapeDtypeStruct((n, PAD, width), f32),
            jax.ShapeDtypeStruct((n, PAD, 128), f32),
        ),
        in_specs=[pl.BlockSpec(memory_space=pl.ANY), vmem, vmem],
        out_specs=(vmem, vmem, vmem),
        scratch_shapes=[
            pltpu.VMEM((n, rows, width), f32),
            pltpu.VMEM((n, PAD, wide), f32),
            pltpu.VMEM((n, PAD, wide), f32),
            pltpu.VMEM((m, PAD, wide), f32),
            pltpu.VMEM((n, PAD, wide), f32),
            pltpu.VMEM((n, PAD, 128), f32),
        ]
        + [dma((n,))] * 6
        + [dma((m,))] * 2
        + [dma((n,))] * 2,
        compiler_params=pltpu.CompilerParams(
            collective_id=0, has_side_effects=True, vmem_limit_bytes=40 * 1024 * 1024
        ),
    )(jacobian, prev_update, energy_tile)


def solve_kernel(n, rows, scale, gram_ref, eall_ref, cent_ref, prev_ref, out_ref):
    wide = n * PAD
    walkers = n * rows
    sub = lax.broadcasted_iota(jnp.int32, (PAD, wide), 0)
    lane = lax.broadcasted_iota(jnp.int32, (PAD, wide), 1)
    real_row = sub < rows
    real = real_row & (lane % PAD < rows)
    energies = [jnp.broadcast_to(eall_ref[i, :, 0:1], (PAD, wide)) for i in range(n)]
    esum = energies[0]
    for i in range(1, n):
        esum = esum + energies[i]
    emean = jnp.sum(jnp.where(real_row, esum, 0.0), axis=0, keepdims=True) * (1.0 / walkers)
    panels = []
    for i in range(n):
        g = gram_ref[i] * scale
        eps = -(energies[i] - emean) * (1.0 / math.sqrt(walkers))
        along = jnp.broadcast_to(g[:, rows : rows + 1], (PAD, wide))
        right = eps - momentum * along
        panel = jnp.where(real, g, 0.0)
        panel = jnp.where(real & (lane == sub + i * PAD), panel + damping, panel)
        panels.append(jnp.where(real_row & (lane == rows), right, panel))

    def spread(panel, column):
        return jnp.broadcast_to(panel[:, column : column + 1], (PAD, wide))

    for g in range(n):
        top = panels[g]
        marks = [spread(top, g * PAD + r) for r in range(rows)]
        for r in range(rows):
            inverse = 1.0 / marks[r][r : r + 1, :]
            here = sub == r
            factor = jnp.where(here, 0.0, marks[r])
            line = top[r : r + 1, :] * inverse
            top = jnp.where(here, line, top - factor * line)
            for q in range(r + 1, rows):
                line_q = marks[q][r : r + 1, :] * inverse
                marks[q] = jnp.where(here, line_q, marks[q] - factor * line_q)
        for i in range(n):
            if i == g:
                continue
            panel = panels[i]
            fresh = panel
            for r in range(rows):
                fresh = fresh - spread(panel, g * PAD + r) * top[r : r + 1, :]
            panels[i] = fresh
        panels[g] = top

    width = cent_ref.shape[2]
    acc = jnp.zeros((PAD, width), jnp.float32)
    keep = lax.broadcasted_iota(jnp.int32, (PAD, width), 0) < rows
    for i in range(n):
        solved = jnp.broadcast_to(panels[i][:, rows : rows + 1], (PAD, width))
        acc = acc + solved * cent_ref[i]
    acc = jnp.where(keep, acc, 0.0)
    out_ref[...] = jnp.sum(acc, axis=0, keepdims=True) + momentum * prev_ref[...]


def solve(n, rows, scale, gram, eall, cent, prev_update):
    if n * PAD <= 128:
        return pl.pallas_call(
            functools.partial(solve_kernel, n, rows, scale),
            out_shape=jax.ShapeDtypeStruct(prev_update.shape, jnp.float32),
            compiler_params=pltpu.CompilerParams(vmem_limit_bytes=40 * 1024 * 1024),
        )(gram, eall, cent, prev_update)
    walkers = n * rows
    along = gram[:, :rows, rows].reshape(walkers) * scale
    square = gram.reshape(n, PAD, n, PAD)[:, :rows, :, :rows].reshape(walkers, walkers) * scale
    energies = eall[:, :rows, 0].reshape(walkers)
    eps = -(energies - jnp.mean(energies)) / math.sqrt(walkers)
    system = square + damping * jnp.eye(walkers, dtype=jnp.float32)
    factor = jnp.linalg.cholesky(system)
    solved = jax.scipy.linalg.cho_solve((factor, True), eps - momentum * along)
    flat = cent[:, :rows, :].reshape(walkers, -1)
    update = jnp.dot(
        solved, flat, precision=lax.Precision.HIGHEST, preferred_element_type=jnp.float32
    )
    return update[None, :] + momentum * prev_update


def body(
    n,
    m,
    jacobian,
    prev_update,
    base_energy,
    elec_pos,
    atom_pos,
    quad_ratio,
    rotation,
    channels,
    ecp_coef,
    ecp_expo,
):
    energy_mine = base_energy + nonlocal_energy(
        elec_pos, atom_pos, quad_ratio, rotation, channels, ecp_coef, ecp_expo
    )
    rows = jacobian.shape[0]
    tile = jnp.zeros((PAD, 128), jnp.float32).at[:rows, :].set(energy_mine[:, None])
    gram, cent, eall = exchange(n, m, jacobian, prev_update, tile)
    scale = 1.0 / (jacobian.shape[1] * m)
    update = solve(n, rows, scale, gram, eall, cent, prev_update)
    return (energy_mine, update)


def solution(mesh):
    in_specs = (
        P("walk", "col"),
        P("col", "walk"),
        P("walk"),
        P("walk", None, None),
        P(),
        P("walk", None, None, None),
        P("walk", None),
        P(),
        P(),
        P(),
    )
    out_specs = (P("walk"), P("col", "walk"))
    run = functools.partial(body, mesh.shape["walk"], mesh.shape["col"])
    return jax.shard_map(run, mesh=mesh, in_specs=in_specs, out_specs=out_specs, check_vma=False)
```

```python
import functools
import math

import jax
import jax.numpy as jnp
from jax import lax
from jax.experimental import pallas as pl
from jax.experimental.pallas import tpu as pltpu
from jax.sharding import PartitionSpec as P

NROT = 16


momentum = 0.9
damping = 0.1


MESH = pl.DeviceIdType.MESH
PAD = 8


def icosa_points():
    golden = (1.0 + math.sqrt(5.0)) / 2.0
    length = math.sqrt(1.0 + golden * golden)
    rows = []
    for first in (-1.0, 1.0):
        for second in (-golden, golden):
            rows.append((0.0, first / length, second / length))
            rows.append((first / length, second / length, 0.0))
            rows.append((second / length, 0.0, first / length))
    return rows


def rotation_table(count):
    points = icosa_points()
    quad = len(points)
    angle = lax.broadcasted_iota(jnp.int32, (1, count), 1).astype(jnp.float32)
    turn_z = 2.0 * math.pi * angle / count
    turn_x = 0.9 * angle
    cz, sz = (jnp.cos(turn_z), jnp.sin(turn_z))
    cx, sx = (jnp.cos(turn_x), jnp.sin(turn_x))
    matrix = [[cz, -sz * cx, sz * sx], [sz, cz * cx, -cz * sx], [jnp.zeros_like(cz), sx, cx]]
    index = lax.broadcasted_iota(jnp.int32, (quad, count), 0)
    place = []
    for d in range(3):
        column = jnp.zeros((quad, count), jnp.float32)
        for j in range(quad):
            column = jnp.where(index == j, points[j][d], column)
        place.append(column)
    return [
        matrix[c][0] * place[0] + matrix[c][1] * place[1] + matrix[c][2] * place[2]
        for c in range(3)
    ]


def as_column(row):
    count = row.shape[1]
    index = lax.broadcasted_iota(jnp.int32, (count, count), 0)
    other = lax.broadcasted_iota(jnp.int32, (count, count), 1)
    return jnp.sum(jnp.where(index == other, row, 0.0), axis=1, keepdims=True)


def walker_energies(elec, atom, quad, rotation, channels, coef, expo, base, out):
    rows, points, atoms, electrons = quad.shape
    lmax = coef.shape[0]
    table = rotation_table(NROT)
    spot = [as_column(atom[c : c + 1, :]) for c in range(3)]
    count = as_column(channels[...].astype(jnp.float32))
    strength = [as_column(coef[level : level + 1, :]) for level in range(lmax)]
    decay = [as_column(expo[level : level + 1, :]) for level in range(lmax)]
    first = as_column(base[...])
    out[...] = jnp.zeros_like(out)
    kind = lax.broadcasted_iota(jnp.int32, (NROT, electrons), 0)

    def walker(w, _):
        onehot = (kind == rotation[pl.ds(w, 1), :]).astype(jnp.float32)
        turned = [
            jnp.dot(
                table[c], onehot, precision=lax.Precision.HIGHEST, preferred_element_type=jnp.float32
            )
            for c in range(3)
        ]
        where = elec[w]
        diff = [where[c : c + 1, :] - spot[c] for c in range(3)]
        dist2 = diff[0] * diff[0] + diff[1] * diff[1] + diff[2] * diff[2]
        root = jnp.sqrt(dist2 + 0.01)
        unit = [d / root for d in diff]
        angular = [jnp.zeros((atoms, electrons), jnp.float32) for _ in range(lmax)]
        for j in range(points):
            ratio = quad[w, j]
            cosang = unit[0] * turned[0][j : j + 1, :]
            cosang = cosang + unit[1] * turned[1][j : j + 1, :]
            cosang = cosang + unit[2] * turned[2][j : j + 1, :]
            lower, upper = None, None
            for level in range(lmax):
                if level == 0:
                    angular[0] = angular[0] + ratio
                    continue
                if level == 1:
                    lower, upper = 1.0, cosang
                else:
                    fresh = ((2 * level - 1) * cosang * upper - (level - 1) * lower) * (1.0 / level)
                    lower, upper = upper, fresh
                angular[level] = angular[level] + upper * ratio
        total = jnp.zeros((atoms, electrons), jnp.float32)
        for level in range(lmax):
            active = (count > level).astype(jnp.float32)
            radial = (strength[level] * active) * jnp.exp(-decay[level] * dist2)
            total = total + ((2 * level + 1) / points) * radial * angular[level]
        value = jnp.sum(jnp.sum(total, axis=1, keepdims=True), axis=0, keepdims=True)
        out[pl.ds(w, 1), :] = jnp.broadcast_to(value, (1, out.shape[1]))
        return 0

    lax.fori_loop(0, rows, walker, 0)
    out[0:rows, :] = out[0:rows, :] + first


def far_first(n):
    order, span = [], n
    while span > 1:
        order += [s for s in range(span // 2, n, span)]
        span //= 2
    return order + [s for s in range(1, n) if s not in order]


def step_kernel(
    n,
    m,
    finish,
    jac_ref,
    prev_ref,
    base_ref,
    elec_ref,
    atom_ref,
    quad_ref,
    rotation_ref,
    channels_ref,
    coef_ref,
    expo_ref,
    *rest,
):
    if finish:
        energy_ref, update_ref = rest[:2]
        rest = rest[2:]
        cent_ref, rest = rest[0], rest[1:]
    else:
        energy_ref, gram_ref, cent_ref = rest[:3]
        rest = rest[3:]
    (
        quad,
        cols,
        part,
        shares,
        pair,
        full,
        energies,
        quad_sem,
        jac_send,
        jac_recv,
        rs_send,
        rs_recv,
        pair_send,
        pair_recv,
        ag_send,
        ag_recv,
    ) = rest
    me = lax.axis_index("walk")
    my_col = lax.axis_index("col")
    rows, width = cols.shape[1:]
    walkers = rows * n
    scale = 1.0 / (width * n * m)
    order = far_first(n)
    fetch = pltpu.make_async_copy(quad_ref, quad, quad_sem)
    fetch.start()

    barrier = pltpu.get_barrier_semaphore()
    for s in order:
        pl.semaphore_signal(
            barrier, inc=1, device_id=(lax.rem(me + s, n), my_col), device_id_type=MESH
        )
    for s in range(1, m):
        pl.semaphore_signal(
            barrier, inc=1, device_id=(me, lax.rem(my_col + s, m)), device_id_type=MESH
        )
    pl.semaphore_wait(barrier, n + m - 2)

    def block(index):
        return jac_ref.at[:, pl.ds(pl.multiple_of(index * width, width), width)]

    def send(src, dst, send_sem, recv_sem, s):
        pltpu.make_async_remote_copy(
            src_ref=src,
            dst_ref=dst.at[me],
            send_sem=send_sem,
            recv_sem=recv_sem,
            device_id=(lax.rem(me + s, n), my_col),
            device_id_type=MESH,
        ).start()

    def wait_bytes(like, sem):
        pltpu.make_async_copy(like, like, sem).wait()

    for s in order:
        send(block(lax.rem(me + s, n)), cols, jac_send, jac_recv, s)
    pltpu.make_async_copy(block(me), cols.at[me], jac_recv).start()

    fetch.wait()
    walker_energies(
        elec_ref, atom_ref, quad, rotation_ref, channels_ref, coef_ref, expo_ref, base_ref, energies
    )
    index = lax.broadcasted_iota(jnp.int32, (rows, rows), 0)
    other = lax.broadcasted_iota(jnp.int32, (rows, rows), 1)
    energy_ref[...] = jnp.sum(
        jnp.where(index == other, energies[0:rows, 0:rows], 0.0), axis=0, keepdims=True
    )
    cent_ref[...] = jnp.zeros_like(cent_ref)
    cent_ref[0, rows : rows + 1, :] = prev_ref[...]

    wait_bytes(cols, jac_recv)
    total = cols[0]
    for i in range(1, n):
        total = total + cols[i]
    mean = jnp.sum(total, axis=0, keepdims=True) * (1.0 / walkers)
    for i in range(n):
        cent_ref[i, 0:rows, :] = cols[i] - mean
    cent = cent_ref[...].reshape(n * PAD, width)
    part[...] = lax.dot_general(
        cent,
        cent,
        (((1,), (1,)), ((), ())),
        precision=lax.Precision.HIGHEST,
        preferred_element_type=jnp.float32,
    ).reshape(part.shape)

    for s in order:
        send(part.at[lax.rem(me + s, n)], shares, rs_send, rs_recv, s)
    shares[me] = part[me]
    wait_bytes(shares.at[pl.ds(0, n - 1)], rs_recv)
    acc = shares[0]
    for i in range(1, n):
        acc = acc + shares[i]
    pair[my_col] = acc

    def pair_copy(s, origin):
        return pltpu.make_async_remote_copy(
            src_ref=pair.at[my_col],
            dst_ref=pair.at[origin],
            send_sem=pair_send.at[s],
            recv_sem=pair_recv.at[origin],
            device_id=(me, lax.rem(my_col + s, m)),
            device_id_type=MESH,
        )

    for s in range(1, m):
        pair_copy(s, my_col).start()
    for s in range(1, m):
        pair_copy(s, lax.rem(my_col + s, m)).wait_recv()
    acc = pair[0]
    for c in range(1, m):
        acc = acc + pair[c]
    lane = lax.broadcasted_iota(jnp.int32, acc.shape, 1)
    spare = jnp.broadcast_to(energies[:, 0:1], acc.shape)
    full[me] = jnp.where(lane == rows + 1, spare, acc * scale)

    for s in order:
        send(full.at[me], full, ag_send, ag_recv, s)
    wait_bytes(full.at[pl.ds(0, n - 1)], ag_recv)
    if finish:
        solve(n, rows, full, cent_ref, prev_ref, update_ref)
    else:
        gram_ref[...] = full[...]

    wait_bytes(cols.at[pl.ds(0, n - 1)], jac_send)
    wait_bytes(part.at[pl.ds(0, n - 1)], rs_send)
    wait_bytes(full.at[pl.ds(0, n - 1)], ag_send)
    for s in range(1, m):
        pair_copy(s, my_col).wait_send()


def solve(n, rows, gram_ref, cent_ref, prev_ref, out_ref):
    wide = n * PAD
    walkers = n * rows
    sub = lax.broadcasted_iota(jnp.int32, (PAD, wide), 0)
    lane = lax.broadcasted_iota(jnp.int32, (PAD, wide), 1)
    real_row = sub < rows
    real = real_row & (lane % PAD < rows)
    energies = [
        jnp.broadcast_to(gram_ref[i][:, rows + 1 : rows + 2], (PAD, wide)) for i in range(n)
    ]
    esum = energies[0]
    for i in range(1, n):
        esum = esum + energies[i]
    emean = jnp.sum(jnp.where(real_row, esum, 0.0), axis=0, keepdims=True) * (1.0 / walkers)
    panels = []
    for i in range(n):
        g = gram_ref[i]
        eps = -(energies[i] - emean) * (1.0 / math.sqrt(walkers))
        along = jnp.broadcast_to(g[:, rows : rows + 1], (PAD, wide))
        right = eps - momentum * along
        panel = jnp.where(real, g, 0.0)
        panel = jnp.where(real & (lane == sub + i * PAD), panel + damping, panel)
        panels.append(jnp.where(real_row & (lane == rows), right, panel))

    def spread(panel, column):
        return jnp.broadcast_to(panel[:, column : column + 1], (PAD, wide))

    for g in range(n):
        top = panels[g]
        marks = [spread(top, g * PAD + r) for r in range(rows)]
        for r in range(rows):
            inverse = 1.0 / marks[r][r : r + 1, :]
            here = sub == r
            factor = jnp.where(here, 0.0, marks[r])
            line = top[r : r + 1, :] * inverse
            top = jnp.where(here, line, top - factor * line)
            for q in range(r + 1, rows):
                line_q = marks[q][r : r + 1, :] * inverse
                marks[q] = jnp.where(here, line_q, marks[q] - factor * line_q)
        for i in range(n):
            if i == g:
                continue
            panel = panels[i]
            fresh = panel
            for r in range(rows):
                fresh = fresh - spread(panel, g * PAD + r) * top[r : r + 1, :]
            panels[i] = fresh
        panels[g] = top

    width = cent_ref.shape[2]
    acc = jnp.zeros((PAD, width), jnp.float32)
    keep = lax.broadcasted_iota(jnp.int32, (PAD, width), 0) < rows
    for i in range(n):
        solved = jnp.broadcast_to(panels[i][:, rows : rows + 1], (PAD, width))
        acc = acc + solved * cent_ref[i]
    acc = jnp.where(keep, acc, 0.0)
    out_ref[...] = jnp.sum(acc, axis=0, keepdims=True) + momentum * prev_ref[...]


def step(n, m, prev_update, jacobian, base, elec_pos, atom_pos, quad, rotation, channels, coef, expo):
    rows = jacobian.shape[0]
    width = jacobian.shape[1] // n
    wide = n * PAD
    finish = wide <= 128
    vmem = pl.BlockSpec(memory_space=pltpu.VMEM)
    anywhere = pl.BlockSpec(memory_space=pl.ANY)
    f32 = jnp.float32
    dma = pltpu.SemaphoreType.DMA
    gram = jax.ShapeDtypeStruct((n, PAD, wide), f32)
    cent = jax.ShapeDtypeStruct((n, PAD, width), f32)
    out_shape = [jax.ShapeDtypeStruct((1, rows), f32)]
    scratch = []
    if finish:
        out_shape += [jax.ShapeDtypeStruct(prev_update.shape, f32)]
        scratch += [pltpu.VMEM(cent.shape, f32)]
    else:
        out_shape += [gram, cent]
    return pl.pallas_call(
        functools.partial(step_kernel, n, m, finish),
        out_shape=out_shape,
        in_specs=[anywhere] + [vmem] * 4 + [anywhere] + [vmem] * 4,
        out_specs=[vmem] * len(out_shape),
        scratch_shapes=scratch
        + [
            pltpu.VMEM(quad.shape, f32),
            pltpu.VMEM((n, rows, width), f32),
            pltpu.VMEM(gram.shape, f32),
            pltpu.VMEM(gram.shape, f32),
            pltpu.VMEM((m, PAD, wide), f32),
            pltpu.VMEM(gram.shape, f32),
            pltpu.VMEM((PAD, 128), f32),
        ]
        + [dma] * 5
        + [dma((m,))] * 2
        + [dma] * 2,
        compiler_params=pltpu.CompilerParams(
            collective_id=0, has_side_effects=True, vmem_limit_bytes=40 * 1024 * 1024
        ),
    )(jacobian, prev_update, base, elec_pos, atom_pos, quad, rotation, channels, coef, expo)


def finish_outside(n, rows, gram, cent, prev_update):
    walkers = n * rows
    along = gram[:, :rows, rows].reshape(walkers)
    energies = gram[:, :rows, rows + 1].reshape(walkers)
    square = gram.reshape(n, PAD, n, PAD)[:, :rows, :, :rows].reshape(walkers, walkers)
    eps = -(energies - jnp.mean(energies)) / math.sqrt(walkers)
    system = square + damping * jnp.eye(walkers, dtype=jnp.float32)
    factor = jnp.linalg.cholesky(system)
    solved = jax.scipy.linalg.cho_solve((factor, True), eps - momentum * along)
    flat = cent[:, :rows, :].reshape(walkers, -1)
    update = jnp.dot(
        solved, flat, precision=lax.Precision.HIGHEST, preferred_element_type=jnp.float32
    )
    return update[None, :] + momentum * prev_update


def body(
    n,
    m,
    jacobian,
    prev_update,
    base_energy,
    elec_pos,
    atom_pos,
    quad_ratio,
    rotation,
    channels,
    ecp_coef,
    ecp_expo,
):
    rows = jacobian.shape[0]
    energy, *rest = step(
        n,
        m,
        prev_update,
        jacobian,
        base_energy.reshape(1, -1),
        elec_pos,
        atom_pos,
        jnp.transpose(quad_ratio, (0, 3, 1, 2)),
        rotation,
        channels.reshape(1, -1),
        ecp_coef.T,
        ecp_expo.T,
    )
    if len(rest) == 1:
        update = rest[0]
    else:
        update = finish_outside(n, rows, *rest, prev_update)
    return (energy.reshape(rows), update)


def solution(mesh):
    in_specs = (
        P("walk", "col"),
        P("col", "walk"),
        P("walk"),
        P("walk", None, None),
        P(),
        P("walk", None, None, None),
        P("walk", None),
        P(),
        P(),
        P(),
    )
    out_specs = (P("walk"), P("col", "walk"))
    run = functools.partial(body, mesh.shape["walk"], mesh.shape["col"])
    return jax.shard_map(run, mesh=mesh, in_specs=in_specs, out_specs=out_specs, check_vma=False)
```

```python
import functools
import math

import jax
import jax.numpy as jnp
from jax import lax
from jax.experimental import pallas as pl
from jax.experimental.pallas import tpu as pltpu
from jax.sharding import PartitionSpec as P

NROT = 16


momentum = 0.9
damping = 0.1


MESH = pl.DeviceIdType.MESH
PAD = 8
CHUNKS = 2


def icosa_points():
    golden = (1.0 + math.sqrt(5.0)) / 2.0
    length = math.sqrt(1.0 + golden * golden)
    rows = []
    for first in (-1.0, 1.0):
        for second in (-golden, golden):
            rows.append((0.0, first / length, second / length))
            rows.append((first / length, second / length, 0.0))
            rows.append((second / length, 0.0, first / length))
    return rows


def rotation_table(count):
    points = icosa_points()
    quad = len(points)
    angle = lax.broadcasted_iota(jnp.int32, (1, count), 1).astype(jnp.float32)
    turn_z = 2.0 * math.pi * angle / count
    turn_x = 0.9 * angle
    cz, sz = (jnp.cos(turn_z), jnp.sin(turn_z))
    cx, sx = (jnp.cos(turn_x), jnp.sin(turn_x))
    matrix = [[cz, -sz * cx, sz * sx], [sz, cz * cx, -cz * sx], [jnp.zeros_like(cz), sx, cx]]
    index = lax.broadcasted_iota(jnp.int32, (quad, count), 0)
    place = []
    for d in range(3):
        column = jnp.zeros((quad, count), jnp.float32)
        for j in range(quad):
            column = jnp.where(index == j, points[j][d], column)
        place.append(column)
    return [
        matrix[c][0] * place[0] + matrix[c][1] * place[1] + matrix[c][2] * place[2]
        for c in range(3)
    ]


def as_column(row):
    count = row.shape[1]
    index = lax.broadcasted_iota(jnp.int32, (count, count), 0)
    other = lax.broadcasted_iota(jnp.int32, (count, count), 1)
    return jnp.sum(jnp.where(index == other, row, 0.0), axis=1, keepdims=True)


def walker_energies(elec, atom, quad, rotation, channels, coef, expo, base, out):
    rows, points, atoms, electrons = quad.shape
    lmax = coef.shape[0]
    table = rotation_table(NROT)
    spot = [as_column(atom[c : c + 1, :]) for c in range(3)]
    count = as_column(channels[...].astype(jnp.float32))
    strength = [as_column(coef[level : level + 1, :]) for level in range(lmax)]
    decay = [as_column(expo[level : level + 1, :]) for level in range(lmax)]
    first = as_column(base[...])
    out[...] = jnp.zeros_like(out)
    kind = lax.broadcasted_iota(jnp.int32, (NROT, electrons), 0)

    def walker(w, _):
        onehot = (kind == rotation[pl.ds(w, 1), :]).astype(jnp.float32)
        turned = [
            jnp.dot(
                table[c], onehot, precision=lax.Precision.HIGHEST, preferred_element_type=jnp.float32
            )
            for c in range(3)
        ]
        where = elec[w]
        diff = [where[c : c + 1, :] - spot[c] for c in range(3)]
        dist2 = diff[0] * diff[0] + diff[1] * diff[1] + diff[2] * diff[2]
        root = jnp.sqrt(dist2 + 0.01)
        unit = [d / root for d in diff]
        angular = [jnp.zeros((atoms, electrons), jnp.float32) for _ in range(lmax)]
        for j in range(points):
            ratio = quad[w, j]
            cosang = unit[0] * turned[0][j : j + 1, :]
            cosang = cosang + unit[1] * turned[1][j : j + 1, :]
            cosang = cosang + unit[2] * turned[2][j : j + 1, :]
            lower, upper = None, None
            for level in range(lmax):
                if level == 0:
                    angular[0] = angular[0] + ratio
                    continue
                if level == 1:
                    lower, upper = 1.0, cosang
                else:
                    fresh = ((2 * level - 1) * cosang * upper - (level - 1) * lower) * (1.0 / level)
                    lower, upper = upper, fresh
                angular[level] = angular[level] + upper * ratio
        total = jnp.zeros((atoms, electrons), jnp.float32)
        for level in range(lmax):
            active = (count > level).astype(jnp.float32)
            radial = (strength[level] * active) * jnp.exp(-decay[level] * dist2)
            total = total + ((2 * level + 1) / points) * radial * angular[level]
        value = jnp.sum(jnp.sum(total, axis=1, keepdims=True), axis=0, keepdims=True)
        out[pl.ds(w, 1), :] = jnp.broadcast_to(value, (1, out.shape[1]))
        return 0

    lax.fori_loop(0, rows, walker, 0)
    out[0:rows, :] = out[0:rows, :] + first


def far_first(n):
    order, span = [], n
    while span > 1:
        order += [s for s in range(span // 2, n, span)]
        span //= 2
    return order + [s for s in range(1, n) if s not in order]


def step_kernel(
    n,
    m,
    finish,
    jac_ref,
    prev_ref,
    base_ref,
    elec_ref,
    atom_ref,
    quad_ref,
    rotation_ref,
    channels_ref,
    coef_ref,
    expo_ref,
    energy_ref,
    result_ref,
    cent_ref,
    prev,
    base,
    elec,
    atom,
    quad,
    rotation,
    channels,
    coef,
    expo,
    cols,
    part,
    shares,
    pair,
    full,
    energies,
    fetch_sem,
    jac_send,
    jac_recv,
    rs_send,
    rs_recv,
    pair_send,
    pair_recv,
    ag_send,
    ag_recv,
):
    me = lax.axis_index("walk")
    my_col = lax.axis_index("col")
    chunks, _, rows, span = cols.shape
    width = chunks * span
    walkers = rows * n
    scale = 1.0 / (width * n * m)
    order = far_first(n)
    barrier = pltpu.get_barrier_semaphore()
    for s in order:
        pl.semaphore_signal(
            barrier, inc=1, device_id=(lax.rem(me + s, n), my_col), device_id_type=MESH
        )
    for s in range(1, m):
        pl.semaphore_signal(
            barrier, inc=1, device_id=(me, lax.rem(my_col + s, m)), device_id_type=MESH
        )
    sources = (
        quad_ref,
        prev_ref,
        base_ref,
        elec_ref,
        atom_ref,
        rotation_ref,
        channels_ref,
        coef_ref,
        expo_ref,
    )
    targets = (quad, prev, base, elec, atom, rotation, channels, coef, expo)
    fetches = [
        pltpu.make_async_copy(source, target, fetch_sem.at[k])
        for k, (source, target) in enumerate(zip(sources, targets))
    ]
    for fetch in fetches:
        fetch.start()
    pl.semaphore_wait(barrier, n + m - 2)

    def block(index, k):
        return jac_ref.at[:, pl.ds(pl.multiple_of(index * width + k * span, span), span)]

    def send(src, dst, send_sem, recv_sem, s):
        pltpu.make_async_remote_copy(
            src_ref=src,
            dst_ref=dst.at[me],
            send_sem=send_sem,
            recv_sem=recv_sem,
            device_id=(lax.rem(me + s, n), my_col),
            device_id_type=MESH,
        ).start()

    def wait_bytes(like, sem):
        pltpu.make_async_copy(like, like, sem).wait()

    for k in range(chunks):
        for s in order:
            send(block(lax.rem(me + s, n), k), cols.at[k], jac_send.at[k], jac_recv.at[k], s)
        pltpu.make_async_copy(block(me, k), cols.at[k, me], jac_recv.at[k]).start()

    for fetch in fetches:
        fetch.wait()
    walker_energies(elec, atom, quad, rotation, channels, coef, expo, base, energies)
    cent_ref[...] = jnp.zeros_like(cent_ref)
    cent_ref[0, rows : rows + 1, :] = prev[...]

    gram = None
    for k in range(chunks):
        wait_bytes(cols.at[k], jac_recv.at[k])
        total = cols[k, 0]
        for i in range(1, n):
            total = total + cols[k, i]
        mean = jnp.sum(total, axis=0, keepdims=True) * (1.0 / walkers)
        for i in range(n):
            cent_ref[i, 0:rows, k * span : (k + 1) * span] = cols[k, i] - mean
        cent = cent_ref[:, :, k * span : (k + 1) * span].reshape(n * PAD, span)
        piece = lax.dot_general(
            cent,
            cent,
            (((1,), (1,)), ((), ())),
            precision=lax.Precision.HIGHEST,
            preferred_element_type=jnp.float32,
        )
        gram = piece if gram is None else gram + piece
    part[...] = gram.reshape(part.shape)

    for s in order:
        send(part.at[lax.rem(me + s, n)], shares, rs_send, rs_recv, s)
    shares[me] = part[me]
    wait_bytes(shares.at[pl.ds(0, n - 1)], rs_recv)
    acc = shares[0]
    for i in range(1, n):
        acc = acc + shares[i]
    pair[my_col] = acc

    def pair_copy(s, origin):
        return pltpu.make_async_remote_copy(
            src_ref=pair.at[my_col],
            dst_ref=pair.at[origin],
            send_sem=pair_send.at[s],
            recv_sem=pair_recv.at[origin],
            device_id=(me, lax.rem(my_col + s, m)),
            device_id_type=MESH,
        )

    for s in range(1, m):
        pair_copy(s, my_col).start()
    for s in range(1, m):
        pair_copy(s, lax.rem(my_col + s, m)).wait_recv()
    acc = pair[0]
    for c in range(1, m):
        acc = acc + pair[c]
    lane = lax.broadcasted_iota(jnp.int32, acc.shape, 1)
    spare = jnp.broadcast_to(energies[:, 0:1], acc.shape)
    full[me] = jnp.where(lane == rows + 1, spare, acc * scale)

    for s in order:
        send(full.at[me], full, ag_send, ag_recv, s)
    wait_bytes(full.at[pl.ds(0, n - 1)], ag_recv)
    if finish:
        solve(n, rows, full, cent_ref, prev, energies, result_ref, energy_ref)
    else:
        result_ref[...] = full[...]
        energy_ref[...] = jnp.broadcast_to(energies[0:rows, 0:1], (rows, 128))

    for k in range(chunks):
        wait_bytes(cols.at[k, pl.ds(0, n - 1)], jac_send.at[k])
    wait_bytes(part.at[pl.ds(0, n - 1)], rs_send)
    wait_bytes(full.at[pl.ds(0, n - 1)], ag_send)
    for s in range(1, m):
        pair_copy(s, my_col).wait_send()


def solve(n, rows, gram_ref, cent_ref, prev_ref, energy_ref, out_ref, mine_ref):
    index = lax.broadcasted_iota(jnp.int32, (rows, rows), 0)
    other = lax.broadcasted_iota(jnp.int32, (rows, rows), 1)
    mine_ref[...] = jnp.sum(
        jnp.where(index == other, energy_ref[0:rows, 0:rows], 0.0), axis=0, keepdims=True
    )
    wide = n * PAD
    walkers = n * rows
    sub = lax.broadcasted_iota(jnp.int32, (PAD, wide), 0)
    lane = lax.broadcasted_iota(jnp.int32, (PAD, wide), 1)
    real_row = sub < rows
    real = real_row & (lane % PAD < rows)
    energies = [
        jnp.broadcast_to(gram_ref[i][:, rows + 1 : rows + 2], (PAD, wide)) for i in range(n)
    ]
    esum = energies[0]
    for i in range(1, n):
        esum = esum + energies[i]
    emean = jnp.sum(jnp.where(real_row, esum, 0.0), axis=0, keepdims=True) * (1.0 / walkers)
    panels = []
    for i in range(n):
        g = gram_ref[i]
        eps = -(energies[i] - emean) * (1.0 / math.sqrt(walkers))
        along = jnp.broadcast_to(g[:, rows : rows + 1], (PAD, wide))
        right = eps - momentum * along
        panel = jnp.where(real, g, 0.0)
        panel = jnp.where(real & (lane == sub + i * PAD), panel + damping, panel)
        panels.append(jnp.where(real_row & (lane == rows), right, panel))

    def spread(panel, column):
        return jnp.broadcast_to(panel[:, column : column + 1], (PAD, wide))

    for g in range(n):
        top = panels[g]
        marks = [spread(top, g * PAD + r) for r in range(rows)]
        for r in range(rows):
            inverse = 1.0 / marks[r][r : r + 1, :]
            here = sub == r
            factor = jnp.where(here, 0.0, marks[r])
            line = top[r : r + 1, :] * inverse
            top = jnp.where(here, line, top - factor * line)
            for q in range(r + 1, rows):
                line_q = marks[q][r : r + 1, :] * inverse
                marks[q] = jnp.where(here, line_q, marks[q] - factor * line_q)
        for i in range(n):
            if i == g:
                continue
            panel = panels[i]
            fresh = panel
            for r in range(rows):
                fresh = fresh - spread(panel, g * PAD + r) * top[r : r + 1, :]
            panels[i] = fresh
        panels[g] = top

    width = cent_ref.shape[2]
    acc = jnp.zeros((PAD, width), jnp.float32)
    keep = lax.broadcasted_iota(jnp.int32, (PAD, width), 0) < rows
    for i in range(n):
        solved = jnp.broadcast_to(panels[i][:, rows : rows + 1], (PAD, width))
        acc = acc + solved * cent_ref[i]
    acc = jnp.where(keep, acc, 0.0)
    out_ref[...] = jnp.sum(acc, axis=0, keepdims=True) + momentum * prev_ref[...]


def step(n, m, jacobian, prev_update, base, elec_pos, atom_pos, quad, rotation, channels, coef, expo):
    rows = jacobian.shape[0]
    width = jacobian.shape[1] // n
    wide = n * PAD
    vmem = pl.BlockSpec(memory_space=pltpu.VMEM)
    hbm = pl.BlockSpec(memory_space=pltpu.HBM)
    f32 = jnp.float32
    dma = pltpu.SemaphoreType.DMA
    small = (prev_update, base, elec_pos, atom_pos, quad, rotation, channels, coef, expo)
    finish = wide <= 128
    gram = (n, PAD, wide)
    cent = (n, PAD, width)
    scratch = [pltpu.VMEM(x.shape, x.dtype) for x in small]
    if finish:
        shapes = [(1, rows), prev_update.shape]
        scratch = [pltpu.VMEM(cent, f32)] + scratch
    else:
        shapes = [(rows, 128), gram, cent]
    return pl.pallas_call(
        functools.partial(step_kernel, n, m, finish),
        out_shape=[jax.ShapeDtypeStruct(shape, f32) for shape in shapes],
        in_specs=[hbm] * 10,
        out_specs=[vmem] * len(shapes),
        scratch_shapes=scratch
        + [
            pltpu.VMEM((CHUNKS, n, rows, width // CHUNKS), f32),
            pltpu.VMEM(gram, f32),
            pltpu.VMEM(gram, f32),
            pltpu.VMEM((m, PAD, wide), f32),
            pltpu.VMEM(gram, f32),
            pltpu.VMEM((PAD, 128), f32),
        ]
        + [dma((len(small),)), dma((CHUNKS,)), dma((CHUNKS,)), dma, dma]
        + [dma((m,))] * 2
        + [dma] * 2,
        compiler_params=pltpu.CompilerParams(collective_id=0, has_side_effects=True, vmem_limit_bytes=60 * 1024 * 1024),
    )(jacobian, *small)


def finish_outside(n, rows, gram, cent, prev_update):
    walkers = n * rows
    along = gram[:, :rows, rows].reshape(walkers)
    energies = gram[:, :rows, rows + 1].reshape(walkers)
    square = gram.reshape(n, PAD, n, PAD)[:, :rows, :, :rows].reshape(walkers, walkers)
    eps = -(energies - jnp.mean(energies)) / math.sqrt(walkers)
    system = square + damping * jnp.eye(walkers, dtype=jnp.float32)
    factor = jnp.linalg.cholesky(system)
    solved = jax.scipy.linalg.cho_solve((factor, True), eps - momentum * along)
    flat = cent[:, :rows, :].reshape(walkers, -1)
    update = jnp.dot(
        solved, flat, precision=lax.Precision.HIGHEST, preferred_element_type=jnp.float32
    )
    return update[None, :] + momentum * prev_update


def body(
    n,
    m,
    jacobian,
    prev_update,
    base_energy,
    elec_pos,
    atom_pos,
    quad_ratio,
    rotation,
    channels,
    ecp_coef,
    ecp_expo,
):
    rows = jacobian.shape[0]
    energy, result, *cent = step(
        n,
        m,
        jacobian,
        prev_update,
        base_energy.reshape(1, -1),
        elec_pos,
        atom_pos,
        jnp.transpose(quad_ratio, (0, 3, 1, 2)),
        rotation,
        channels.reshape(1, -1),
        ecp_coef.T,
        ecp_expo.T,
    )
    if cent:
        return (energy[:, 0], finish_outside(n, rows, result, cent[0], prev_update))
    return (energy.reshape(rows), result)


def solution(mesh):
    in_specs = (
        P("walk", "col"),
        P("col", "walk"),
        P("walk"),
        P("walk", None, None),
        P(),
        P("walk", None, None, None),
        P("walk", None),
        P(),
        P(),
        P(),
    )
    out_specs = (P("walk"), P("col", "walk"))
    run = functools.partial(body, mesh.shape["walk"], mesh.shape["col"])
    return jax.shard_map(run, mesh=mesh, in_specs=in_specs, out_specs=out_specs, check_vma=False)
```

```python
import functools
import math

import jax
import jax.numpy as jnp
from jax import lax
from jax.experimental import pallas as pl
from jax.experimental.pallas import tpu as pltpu
from jax.sharding import PartitionSpec as P

NROT = 16


momentum = 0.9
damping = 0.1


MESH = pl.DeviceIdType.MESH
PAD = 8
CHUNKS = 2


def icosa_points():
    golden = (1.0 + math.sqrt(5.0)) / 2.0
    length = math.sqrt(1.0 + golden * golden)
    rows = []
    for first in (-1.0, 1.0):
        for second in (-golden, golden):
            rows.append((0.0, first / length, second / length))
            rows.append((first / length, second / length, 0.0))
            rows.append((second / length, 0.0, first / length))
    return rows


def rotation_table(count):
    points = icosa_points()
    quad = len(points)
    angle = lax.broadcasted_iota(jnp.int32, (1, count), 1).astype(jnp.float32)
    turn_z = 2.0 * math.pi * angle / count
    turn_x = 0.9 * angle
    cz, sz = (jnp.cos(turn_z), jnp.sin(turn_z))
    cx, sx = (jnp.cos(turn_x), jnp.sin(turn_x))
    matrix = [[cz, -sz * cx, sz * sx], [sz, cz * cx, -cz * sx], [jnp.zeros_like(cz), sx, cx]]
    index = lax.broadcasted_iota(jnp.int32, (quad, count), 0)
    place = []
    for d in range(3):
        column = jnp.zeros((quad, count), jnp.float32)
        for j in range(quad):
            column = jnp.where(index == j, points[j][d], column)
        place.append(column)
    return [
        matrix[c][0] * place[0] + matrix[c][1] * place[1] + matrix[c][2] * place[2]
        for c in range(3)
    ]


def as_column(row):
    count = row.shape[1]
    index = lax.broadcasted_iota(jnp.int32, (count, count), 0)
    other = lax.broadcasted_iota(jnp.int32, (count, count), 1)
    return jnp.sum(jnp.where(index == other, row, 0.0), axis=1, keepdims=True)


def walker_energies(share, begin, elec, atom, quad, rotation, channels, coef, expo, base, out):
    rows, points, atoms, electrons = quad.shape
    lmax = coef.shape[0]
    table = rotation_table(NROT)
    spot = [as_column(atom[c : c + 1, :]) for c in range(3)]
    count = as_column(channels[...].astype(jnp.float32))
    strength = [as_column(coef[level : level + 1, :]) for level in range(lmax)]
    decay = [as_column(expo[level : level + 1, :]) for level in range(lmax)]
    first = as_column(base[...])
    out[...] = jnp.zeros_like(out)
    kind = lax.broadcasted_iota(jnp.int32, (NROT, electrons), 0)

    def walker(k, _):
        w = lax.rem(begin + k, rows)
        onehot = (kind == rotation[pl.ds(w, 1), :]).astype(jnp.float32)
        turned = [
            jnp.dot(
                table[c], onehot, precision=lax.Precision.HIGHEST, preferred_element_type=jnp.float32
            )
            for c in range(3)
        ]
        where = elec[w]
        diff = [where[c : c + 1, :] - spot[c] for c in range(3)]
        dist2 = diff[0] * diff[0] + diff[1] * diff[1] + diff[2] * diff[2]
        root = jnp.sqrt(dist2 + 0.01)
        unit = [d / root for d in diff]
        angular = [jnp.zeros((atoms, electrons), jnp.float32) for _ in range(lmax)]
        for j in range(points):
            ratio = quad[w, j]
            cosang = unit[0] * turned[0][j : j + 1, :]
            cosang = cosang + unit[1] * turned[1][j : j + 1, :]
            cosang = cosang + unit[2] * turned[2][j : j + 1, :]
            lower, upper = None, None
            for level in range(lmax):
                if level == 0:
                    angular[0] = angular[0] + ratio
                    continue
                if level == 1:
                    lower, upper = 1.0, cosang
                else:
                    fresh = ((2 * level - 1) * cosang * upper - (level - 1) * lower) * (1.0 / level)
                    lower, upper = upper, fresh
                angular[level] = angular[level] + upper * ratio
        total = jnp.zeros((atoms, electrons), jnp.float32)
        for level in range(lmax):
            active = (count > level).astype(jnp.float32)
            radial = (strength[level] * active) * jnp.exp(-decay[level] * dist2)
            total = total + ((2 * level + 1) / points) * radial * angular[level]
        value = jnp.sum(jnp.sum(total, axis=1, keepdims=True), axis=0, keepdims=True)
        out[pl.ds(w, 1), :] = jnp.broadcast_to(value, (1, out.shape[1]))
        return 0

    lax.fori_loop(0, share, walker, 0)
    place = lax.broadcasted_iota(jnp.int32, (rows, out.shape[1]), 0)
    mine = (place >= begin) & (place < begin + share)
    out[0:rows, :] = jnp.where(mine, out[0:rows, :] + first, 0.0)


def far_first(n):
    order, span = [], n
    while span > 1:
        order += [s for s in range(span // 2, n, span)]
        span //= 2
    return order + [s for s in range(1, n) if s not in order]


def plane_of(n, m):
    flat = 4 if n % 4 == 0 else 1
    while n % (flat * m) != 0:
        flat -= 1
    return flat


def spread_energy(full, me, rows):
    return jnp.broadcast_to(full[me][0:rows, rows + 1 : rows + 2], (rows, 128))


def step_kernel(
    n,
    m,
    finish,
    jac_ref,
    prev_ref,
    base_ref,
    elec_ref,
    atom_ref,
    quad_ref,
    rotation_ref,
    channels_ref,
    coef_ref,
    expo_ref,
    energy_ref,
    result_ref,
    cent_ref,
    prev,
    base,
    elec,
    atom,
    quad,
    rotation,
    channels,
    coef,
    expo,
    cols,
    part,
    shares,
    lines,
    full,
    energies,
    fetch_sem,
    jac_send,
    jac_recv,
    rs_send,
    rs_recv,
    line_send,
    line_recv,
    ag_send,
    ag_recv,
):
    me = lax.axis_index("walk")
    my_col = lax.axis_index("col")
    chunks, _, rows, span = cols.shape
    width = chunks * span
    walkers = rows * n
    scale = 1.0 / (width * n * m)
    order = far_first(n)
    flat = plane_of(n, m)
    plane = flat * m
    groups = n // plane
    layer = me // flat
    inner = lax.rem(me, flat)
    rank = inner * m + my_col
    own = pl.ds(rank * groups, groups)

    barrier = pltpu.get_barrier_semaphore()
    for s in order:
        pl.semaphore_signal(
            barrier, inc=1, device_id=(lax.rem(me + s, n), my_col), device_id_type=MESH
        )
    for s in range(flat):
        for t in range(1, m):
            pl.semaphore_signal(
                barrier,
                inc=1,
                device_id=(layer * flat + lax.rem(inner + s, flat), lax.rem(my_col + t, m)),
                device_id_type=MESH,
            )
    sources = (
        quad_ref,
        prev_ref,
        base_ref,
        elec_ref,
        atom_ref,
        rotation_ref,
        channels_ref,
        coef_ref,
        expo_ref,
    )
    targets = (quad, prev, base, elec, atom, rotation, channels, coef, expo)
    fetches = [
        pltpu.make_async_copy(source, target, fetch_sem.at[k])
        for k, (source, target) in enumerate(zip(sources, targets))
    ]
    for fetch in fetches:
        fetch.start()
    pl.semaphore_wait(barrier, n - 1 + flat * (m - 1))

    def block(index, k):
        return jac_ref.at[:, pl.ds(pl.multiple_of(index * width + k * span, span), span)]

    def send(src, dst, send_sem, recv_sem, s):
        pltpu.make_async_remote_copy(
            src_ref=src,
            dst_ref=dst.at[me],
            send_sem=send_sem,
            recv_sem=recv_sem,
            device_id=(lax.rem(me + s, n), my_col),
            device_id_type=MESH,
        ).start()

    def wait_bytes(like, sem):
        pltpu.make_async_copy(like, like, sem).wait()

    for k in range(chunks):
        for s in order:
            send(block(lax.rem(me + s, n), k), cols.at[k], jac_send.at[k], jac_recv.at[k], s)
        pltpu.make_async_copy(block(me, k), cols.at[k, me], jac_recv.at[k]).start()

    for fetch in fetches:
        fetch.wait()
    share = -(-rows // m)
    walker_energies(share, my_col * share, elec, atom, quad, rotation, channels, coef, expo, base, energies)
    cent_ref[...] = jnp.zeros_like(cent_ref)
    cent_ref[0, rows : rows + 1, :] = prev[...]

    gram = None
    for k in range(chunks):
        wait_bytes(cols.at[k], jac_recv.at[k])
        total = cols[k, 0]
        for i in range(1, n):
            total = total + cols[k, i]
        mean = jnp.sum(total, axis=0, keepdims=True) * (1.0 / walkers)
        for i in range(n):
            cent_ref[i, 0:rows, k * span : (k + 1) * span] = cols[k, i] - mean
        cent = cent_ref[:, :, k * span : (k + 1) * span].reshape(n * PAD, span)
        piece = lax.dot_general(
            cent,
            cent,
            (((1,), (1,)), ((), ())),
            precision=lax.Precision.HIGHEST,
            preferred_element_type=jnp.float32,
        )
        gram = piece if gram is None else gram + piece
    part[...] = (gram * scale).reshape(part.shape)
    lane = lax.broadcasted_iota(jnp.int32, part.shape[1:], 1)
    spare = jnp.broadcast_to(energies[:, 0:1], part.shape[1:])
    part[me] = jnp.where(lane == rows + 1, spare, part[me])

    def peer(s, t):
        return lax.rem(inner + s, flat), lax.rem(my_col + t, m)

    def send_plane(src, dst, send_sem, recv_sem, s, t):
        there, core = peer(s, t)
        pltpu.make_async_remote_copy(
            src_ref=src,
            dst_ref=dst,
            send_sem=send_sem,
            recv_sem=recv_sem,
            device_id=(layer * flat + there, core),
            device_id_type=MESH,
        ).start()

    others = [(s, t) for s in reversed(range(flat)) for t in range(m) if (s, t) != (0, 0)]
    for s, t in others:
        there, core = peer(s, t)
        src = part.at[pl.ds((there * m + core) * groups, groups)]
        send_plane(src, shares.at[rank], rs_send, rs_recv, s, t)
    shares[rank] = part[own]
    wait_bytes(shares.at[pl.ds(0, plane - 1)], rs_recv)
    acc = shares[0]
    for i in range(1, plane):
        acc = acc + shares[i]
    layers = n // flat
    lines[layer] = acc
    for s in range(1, layers):
        pltpu.make_async_remote_copy(
            src_ref=lines.at[layer],
            dst_ref=lines.at[layer],
            send_sem=line_send,
            recv_sem=line_recv,
            device_id=(lax.rem(layer + s, layers) * flat + inner, my_col),
            device_id_type=MESH,
        ).start()
    wait_bytes(lines.at[pl.ds(0, layers - 1)], line_recv)
    acc = lines[0]
    for i in range(1, layers):
        acc = acc + lines[i]
    full[own] = acc
    for s, t in others:
        send_plane(full.at[own], full.at[own], ag_send, ag_recv, s, t)
    wait_bytes(full.at[pl.ds(0, (plane - 1) * groups)], ag_recv)
    if finish:
        solve(n, rows, full, cent_ref, prev, spread_energy(full, me, rows), result_ref, energy_ref)
    else:
        result_ref[...] = full[...]
        energy_ref[...] = spread_energy(full, me, rows)

    for k in range(chunks):
        wait_bytes(cols.at[k, pl.ds(0, n - 1)], jac_send.at[k])
    wait_bytes(shares.at[pl.ds(0, plane - 1)], rs_send)
    wait_bytes(lines.at[pl.ds(0, layers - 1)], line_send)
    wait_bytes(full.at[pl.ds(0, (plane - 1) * groups)], ag_send)


def solve(n, rows, gram_ref, cent_ref, prev_ref, energy_ref, out_ref, mine_ref):
    index = lax.broadcasted_iota(jnp.int32, (rows, rows), 0)
    other = lax.broadcasted_iota(jnp.int32, (rows, rows), 1)
    mine_ref[...] = jnp.sum(
        jnp.where(index == other, energy_ref[:, 0:rows], 0.0), axis=0, keepdims=True
    )
    wide = n * PAD
    walkers = n * rows
    sub = lax.broadcasted_iota(jnp.int32, (PAD, wide), 0)
    lane = lax.broadcasted_iota(jnp.int32, (PAD, wide), 1)
    real_row = sub < rows
    real = real_row & (lane % PAD < rows)
    energies = [
        jnp.broadcast_to(gram_ref[i][:, rows + 1 : rows + 2], (PAD, wide)) for i in range(n)
    ]
    esum = energies[0]
    for i in range(1, n):
        esum = esum + energies[i]
    emean = jnp.sum(jnp.where(real_row, esum, 0.0), axis=0, keepdims=True) * (1.0 / walkers)
    panels = []
    for i in range(n):
        g = gram_ref[i]
        eps = -(energies[i] - emean) * (1.0 / math.sqrt(walkers))
        along = jnp.broadcast_to(g[:, rows : rows + 1], (PAD, wide))
        right = eps - momentum * along
        panel = jnp.where(real, g, 0.0)
        panel = jnp.where(real & (lane == sub + i * PAD), panel + damping, panel)
        panels.append(jnp.where(real_row & (lane == rows), right, panel))

    def spread(panel, column):
        return jnp.broadcast_to(panel[:, column : column + 1], (PAD, wide))

    for g in range(n):
        top = panels[g]
        marks = [spread(top, g * PAD + r) for r in range(rows)]
        for r in range(rows):
            inverse = 1.0 / marks[r][r : r + 1, :]
            here = sub == r
            factor = jnp.where(here, 0.0, marks[r])
            line = top[r : r + 1, :] * inverse
            top = jnp.where(here, line, top - factor * line)
            for q in range(r + 1, rows):
                line_q = marks[q][r : r + 1, :] * inverse
                marks[q] = jnp.where(here, line_q, marks[q] - factor * line_q)
        for i in range(n):
            if i == g:
                continue
            panel = panels[i]
            fresh = panel
            for r in range(rows):
                fresh = fresh - spread(panel, g * PAD + r) * top[r : r + 1, :]
            panels[i] = fresh
        panels[g] = top

    width = cent_ref.shape[2]
    acc = jnp.zeros((PAD, width), jnp.float32)
    keep = lax.broadcasted_iota(jnp.int32, (PAD, width), 0) < rows
    for i in range(n):
        solved = jnp.broadcast_to(panels[i][:, rows : rows + 1], (PAD, width))
        acc = acc + solved * cent_ref[i]
    acc = jnp.where(keep, acc, 0.0)
    out_ref[...] = jnp.sum(acc, axis=0, keepdims=True) + momentum * prev_ref[...]


def step(n, m, jacobian, prev_update, base, elec_pos, atom_pos, quad, rotation, channels, coef, expo):
    rows = jacobian.shape[0]
    width = jacobian.shape[1] // n
    wide = n * PAD
    vmem = pl.BlockSpec(memory_space=pltpu.VMEM)
    hbm = pl.BlockSpec(memory_space=pltpu.HBM)
    f32 = jnp.float32
    dma = pltpu.SemaphoreType.DMA
    small = (prev_update, base, elec_pos, atom_pos, quad, rotation, channels, coef, expo)
    finish = wide <= 128
    flat = plane_of(n, m)
    gram = (n, PAD, wide)
    cent = (n, PAD, width)
    scratch = [pltpu.VMEM(x.shape, x.dtype) for x in small]
    if finish:
        shapes = [(1, rows), prev_update.shape]
        scratch = [pltpu.VMEM(cent, f32)] + scratch
    else:
        shapes = [(rows, 128), gram, cent]
    return pl.pallas_call(
        functools.partial(step_kernel, n, m, finish),
        out_shape=[jax.ShapeDtypeStruct(shape, f32) for shape in shapes],
        in_specs=[hbm] * 10,
        out_specs=[vmem] * len(shapes),
        scratch_shapes=scratch
        + [
            pltpu.VMEM((CHUNKS, n, rows, width // CHUNKS), f32),
            pltpu.VMEM(gram, f32),
            pltpu.VMEM((flat * m, n // (flat * m), PAD, wide), f32),
            pltpu.VMEM((n // flat, n // (flat * m), PAD, wide), f32),
            pltpu.VMEM(gram, f32),
            pltpu.VMEM((PAD, 128), f32),
        ]
        + [dma((len(small),)), dma((CHUNKS,)), dma((CHUNKS,))]
        + [dma] * 6,
        compiler_params=pltpu.CompilerParams(collective_id=0, has_side_effects=True, vmem_limit_bytes=60 * 1024 * 1024),
    )(jacobian, *small)


def finish_outside(n, rows, gram, cent, prev_update):
    walkers = n * rows
    along = gram[:, :rows, rows].reshape(walkers)
    energies = gram[:, :rows, rows + 1].reshape(walkers)
    square = gram.reshape(n, PAD, n, PAD)[:, :rows, :, :rows].reshape(walkers, walkers)
    eps = -(energies - jnp.mean(energies)) / math.sqrt(walkers)
    system = square + damping * jnp.eye(walkers, dtype=jnp.float32)
    factor = jnp.linalg.cholesky(system)
    solved = jax.scipy.linalg.cho_solve((factor, True), eps - momentum * along)
    flat = cent[:, :rows, :].reshape(walkers, -1)
    update = jnp.dot(
        solved, flat, precision=lax.Precision.HIGHEST, preferred_element_type=jnp.float32
    )
    return update[None, :] + momentum * prev_update


def body(
    n,
    m,
    jacobian,
    prev_update,
    base_energy,
    elec_pos,
    atom_pos,
    quad_ratio,
    rotation,
    channels,
    ecp_coef,
    ecp_expo,
):
    rows = jacobian.shape[0]
    energy, result, *cent = step(
        n,
        m,
        jacobian,
        prev_update,
        base_energy.reshape(1, -1),
        elec_pos,
        atom_pos,
        jnp.transpose(quad_ratio, (0, 3, 1, 2)),
        rotation,
        channels.reshape(1, -1),
        ecp_coef.T,
        ecp_expo.T,
    )
    if cent:
        return (energy[:, 0], finish_outside(n, rows, result, cent[0], prev_update))
    return (energy.reshape(rows), result)


def solution(mesh):
    in_specs = (
        P("walk", "col"),
        P("col", "walk"),
        P("walk"),
        P("walk", None, None),
        P(),
        P("walk", None, None, None),
        P("walk", None),
        P(),
        P(),
        P(),
    )
    out_specs = (P("walk"), P("col", "walk"))
    run = functools.partial(body, mesh.shape["walk"], mesh.shape["col"])
    return jax.shard_map(run, mesh=mesh, in_specs=in_specs, out_specs=out_specs, check_vma=False)
```

```python
import functools
import math

import jax
import jax.numpy as jnp
from jax import lax
from jax.experimental import pallas as pl
from jax.experimental.pallas import tpu as pltpu
from jax.sharding import PartitionSpec as P

NROT = 16


momentum = 0.9
damping = 0.1


MESH = pl.DeviceIdType.MESH
PAD = 8


def icosa_points():
    golden = (1.0 + math.sqrt(5.0)) / 2.0
    length = math.sqrt(1.0 + golden * golden)
    rows = []
    for first in (-1.0, 1.0):
        for second in (-golden, golden):
            rows.append((0.0, first / length, second / length))
            rows.append((first / length, second / length, 0.0))
            rows.append((second / length, 0.0, first / length))
    return rows


def rotation_table(count):
    points = icosa_points()
    quad = len(points)
    angle = lax.broadcasted_iota(jnp.int32, (1, count), 1).astype(jnp.float32)
    turn_z = 2.0 * math.pi * angle / count
    turn_x = 0.9 * angle
    cz, sz = (jnp.cos(turn_z), jnp.sin(turn_z))
    cx, sx = (jnp.cos(turn_x), jnp.sin(turn_x))
    matrix = [[cz, -sz * cx, sz * sx], [sz, cz * cx, -cz * sx], [jnp.zeros_like(cz), sx, cx]]
    index = lax.broadcasted_iota(jnp.int32, (quad, count), 0)
    place = []
    for d in range(3):
        column = jnp.zeros((quad, count), jnp.float32)
        for j in range(quad):
            column = jnp.where(index == j, points[j][d], column)
        place.append(column)
    return [
        matrix[c][0] * place[0] + matrix[c][1] * place[1] + matrix[c][2] * place[2]
        for c in range(3)
    ]


def as_column(row):
    count = row.shape[1]
    index = lax.broadcasted_iota(jnp.int32, (count, count), 0)
    other = lax.broadcasted_iota(jnp.int32, (count, count), 1)
    return jnp.sum(jnp.where(index == other, row, 0.0), axis=1, keepdims=True)


def walker_energies(share, begin, elec, atom, quad, rotation, channels, coef, expo, base, out):
    rows, points, atoms, electrons = quad.shape
    lmax = coef.shape[0]
    table = rotation_table(NROT)
    spot = [as_column(atom[c : c + 1, :]) for c in range(3)]
    count = as_column(channels[...].astype(jnp.float32))
    strength = [as_column(coef[level : level + 1, :]) for level in range(lmax)]
    decay = [as_column(expo[level : level + 1, :]) for level in range(lmax)]
    first = as_column(base[...])
    out[...] = jnp.zeros_like(out)
    kind = lax.broadcasted_iota(jnp.int32, (NROT, electrons), 0)

    def walker(k, _):
        w = lax.rem(begin + k, rows)
        onehot = (kind == rotation[pl.ds(w, 1), :]).astype(jnp.float32)
        turned = [
            jnp.dot(
                table[c], onehot, precision=lax.Precision.HIGHEST, preferred_element_type=jnp.float32
            )
            for c in range(3)
        ]
        where = elec[w]
        diff = [where[c : c + 1, :] - spot[c] for c in range(3)]
        dist2 = diff[0] * diff[0] + diff[1] * diff[1] + diff[2] * diff[2]
        root = jnp.sqrt(dist2 + 0.01)
        unit = [d / root for d in diff]
        angular = [jnp.zeros((atoms, electrons), jnp.float32) for _ in range(lmax)]
        for j in range(points):
            ratio = quad[w, j]
            cosang = unit[0] * turned[0][j : j + 1, :]
            cosang = cosang + unit[1] * turned[1][j : j + 1, :]
            cosang = cosang + unit[2] * turned[2][j : j + 1, :]
            lower, upper = None, None
            for level in range(lmax):
                if level == 0:
                    angular[0] = angular[0] + ratio
                    continue
                if level == 1:
                    lower, upper = 1.0, cosang
                else:
                    fresh = ((2 * level - 1) * cosang * upper - (level - 1) * lower) * (1.0 / level)
                    lower, upper = upper, fresh
                angular[level] = angular[level] + upper * ratio
        total = jnp.zeros((atoms, electrons), jnp.float32)
        for level in range(lmax):
            active = (count > level).astype(jnp.float32)
            radial = (strength[level] * active) * jnp.exp(-decay[level] * dist2)
            total = total + ((2 * level + 1) / points) * radial * angular[level]
        value = jnp.sum(jnp.sum(total, axis=1, keepdims=True), axis=0, keepdims=True)
        out[pl.ds(w, 1), :] = jnp.broadcast_to(value, (1, out.shape[1]))
        return 0

    lax.fori_loop(0, share, walker, 0)
    place = lax.broadcasted_iota(jnp.int32, (rows, out.shape[1]), 0)
    mine = (place >= begin) & (place < begin + share)
    out[0:rows, :] = jnp.where(mine, out[0:rows, :] + first, 0.0)


def plane_of(n, m):
    flat = 4 if n % 4 == 0 else 1
    while n % (flat * m) != 0:
        flat -= 1
    return flat


def spread_energy(full, me, rows):
    return jnp.broadcast_to(full[me][0:rows, rows + 1 : rows + 2], (rows, 128))


def energy_kernel(m, elec, atom, quad, rotation, channels, coef, expo, base, energies):
    rows = quad.shape[0]
    share = -(-rows // m)
    begin = lax.axis_index("col") * share
    walker_energies(share, begin, elec, atom, quad, rotation, channels, coef, expo, base, energies)


def step_kernel(
    n,
    m,
    finish,
    cols,
    energies,
    prev,
    energy_ref,
    result_ref,
    cent_ref,
    part,
    shares,
    lines,
    full,
    rs_send,
    rs_recv,
    line_send,
    line_recv,
    ag_send,
    ag_recv,
):
    me = lax.axis_index("walk")
    my_col = lax.axis_index("col")
    _, rows, width = cols.shape
    walkers = rows * n
    scale = 1.0 / (width * n * m)
    flat = plane_of(n, m)
    plane = flat * m
    groups = n // plane
    layer = me // flat
    inner = lax.rem(me, flat)
    rank = inner * m + my_col
    own = pl.ds(rank * groups, groups)

    barrier = pltpu.get_barrier_semaphore()
    layers = n // flat
    others = [(s, t) for s in reversed(range(flat)) for t in range(m) if (s, t) != (0, 0)]
    for s, t in others:
        there, core = lax.rem(inner + s, flat), lax.rem(my_col + t, m)
        pl.semaphore_signal(
            barrier, inc=1, device_id=(layer * flat + there, core), device_id_type=MESH
        )
    for s in range(1, layers):
        there = lax.rem(layer + s, layers) * flat + inner
        pl.semaphore_signal(barrier, inc=1, device_id=(there, my_col), device_id_type=MESH)

    def wait_bytes(like, sem):
        pltpu.make_async_copy(like, like, sem).wait()

    cent_ref[...] = jnp.zeros_like(cent_ref)
    cent_ref[0, rows : rows + 1, :] = prev[...]

    total = cols[0]
    for i in range(1, n):
        total = total + cols[i]
    mean = jnp.sum(total, axis=0, keepdims=True) * (1.0 / walkers)
    for i in range(n):
        cent_ref[i, 0:rows, :] = cols[i] - mean
    cent = cent_ref[...].reshape(n * PAD, width)
    gram = lax.dot_general(
        cent,
        cent,
        (((1,), (1,)), ((), ())),
        precision=lax.Precision.HIGHEST,
        preferred_element_type=jnp.float32,
    )
    part[...] = (gram * scale).reshape(part.shape)
    lane = lax.broadcasted_iota(jnp.int32, part.shape[1:], 1)
    spare = jnp.broadcast_to(energies[:, 0:1], part.shape[1:])
    part[me] = jnp.where(lane == rows + 1, spare, part[me])

    def peer(s, t):
        return lax.rem(inner + s, flat), lax.rem(my_col + t, m)

    def send_plane(src, dst, send_sem, recv_sem, s, t):
        there, core = peer(s, t)
        pltpu.make_async_remote_copy(
            src_ref=src,
            dst_ref=dst,
            send_sem=send_sem,
            recv_sem=recv_sem,
            device_id=(layer * flat + there, core),
            device_id_type=MESH,
        ).start()

    pl.semaphore_wait(barrier, len(others) + layers - 1)
    for s, t in others:
        there, core = peer(s, t)
        src = part.at[pl.ds((there * m + core) * groups, groups)]
        send_plane(src, shares.at[rank], rs_send, rs_recv, s, t)
    shares[rank] = part[own]
    wait_bytes(shares.at[pl.ds(0, plane - 1)], rs_recv)
    acc = shares[0]
    for i in range(1, plane):
        acc = acc + shares[i]
    lines[layer] = acc
    for s in range(1, layers):
        pltpu.make_async_remote_copy(
            src_ref=lines.at[layer],
            dst_ref=lines.at[layer],
            send_sem=line_send,
            recv_sem=line_recv,
            device_id=(lax.rem(layer + s, layers) * flat + inner, my_col),
            device_id_type=MESH,
        ).start()
    wait_bytes(lines.at[pl.ds(0, layers - 1)], line_recv)
    acc = lines[0]
    for i in range(1, layers):
        acc = acc + lines[i]
    full[own] = acc
    for s, t in others:
        send_plane(full.at[own], full.at[own], ag_send, ag_recv, s, t)
    wait_bytes(full.at[pl.ds(0, (plane - 1) * groups)], ag_recv)
    if finish:
        solve(n, rows, full, cent_ref, prev, spread_energy(full, me, rows), result_ref, energy_ref)
    else:
        result_ref[...] = full[...]
        energy_ref[...] = spread_energy(full, me, rows)

    wait_bytes(shares.at[pl.ds(0, plane - 1)], rs_send)
    wait_bytes(lines.at[pl.ds(0, layers - 1)], line_send)
    wait_bytes(full.at[pl.ds(0, (plane - 1) * groups)], ag_send)


def solve(n, rows, gram_ref, cent_ref, prev_ref, energy_ref, out_ref, mine_ref):
    index = lax.broadcasted_iota(jnp.int32, (rows, rows), 0)
    other = lax.broadcasted_iota(jnp.int32, (rows, rows), 1)
    mine_ref[...] = jnp.sum(
        jnp.where(index == other, energy_ref[:, 0:rows], 0.0), axis=0, keepdims=True
    )
    wide = n * PAD
    walkers = n * rows
    sub = lax.broadcasted_iota(jnp.int32, (PAD, wide), 0)
    lane = lax.broadcasted_iota(jnp.int32, (PAD, wide), 1)
    real_row = sub < rows
    real = real_row & (lane % PAD < rows)
    energies = [
        jnp.broadcast_to(gram_ref[i][:, rows + 1 : rows + 2], (PAD, wide)) for i in range(n)
    ]
    esum = energies[0]
    for i in range(1, n):
        esum = esum + energies[i]
    emean = jnp.sum(jnp.where(real_row, esum, 0.0), axis=0, keepdims=True) * (1.0 / walkers)
    panels = []
    for i in range(n):
        g = gram_ref[i]
        eps = -(energies[i] - emean) * (1.0 / math.sqrt(walkers))
        along = jnp.broadcast_to(g[:, rows : rows + 1], (PAD, wide))
        right = eps - momentum * along
        panel = jnp.where(real, g, 0.0)
        panel = jnp.where(real & (lane == sub + i * PAD), panel + damping, panel)
        panels.append(jnp.where(real_row & (lane == rows), right, panel))

    def spread(panel, column):
        return jnp.broadcast_to(panel[:, column : column + 1], (PAD, wide))

    for g in range(n):
        top = panels[g]
        marks = [spread(top, g * PAD + r) for r in range(rows)]
        for r in range(rows):
            inverse = 1.0 / marks[r][r : r + 1, :]
            here = sub == r
            factor = jnp.where(here, 0.0, marks[r])
            line = top[r : r + 1, :] * inverse
            top = jnp.where(here, line, top - factor * line)
            for q in range(r + 1, rows):
                line_q = marks[q][r : r + 1, :] * inverse
                marks[q] = jnp.where(here, line_q, marks[q] - factor * line_q)
        for i in range(n):
            if i == g:
                continue
            panel = panels[i]
            fresh = panel
            for r in range(rows):
                fresh = fresh - spread(panel, g * PAD + r) * top[r : r + 1, :]
            panels[i] = fresh
        panels[g] = top

    width = cent_ref.shape[2]
    acc = jnp.zeros((PAD, width), jnp.float32)
    keep = lax.broadcasted_iota(jnp.int32, (PAD, width), 0) < rows
    for i in range(n):
        solved = jnp.broadcast_to(panels[i][:, rows : rows + 1], (PAD, width))
        acc = acc + solved * cent_ref[i]
    acc = jnp.where(keep, acc, 0.0)
    out_ref[...] = jnp.sum(acc, axis=0, keepdims=True) + momentum * prev_ref[...]


def walkers_mine(m, elec_pos, atom_pos, quad, rotation, channels, coef, expo, base):
    return pl.pallas_call(
        functools.partial(energy_kernel, m),
        out_shape=jax.ShapeDtypeStruct((PAD, 128), jnp.float32),
        compiler_params=pltpu.CompilerParams(vmem_limit_bytes=32 * 1024 * 1024),
        cost_estimate=pl.CostEstimate(
            flops=30 * quad.size, bytes_accessed=4 * quad.size, transcendentals=quad.size
        ),
    )(elec_pos, atom_pos, quad, rotation, channels, coef, expo, base)


def step(n, m, cols, energies, prev_update):
    _, rows, width = cols.shape
    wide = n * PAD
    vmem = pl.BlockSpec(memory_space=pltpu.VMEM)
    f32 = jnp.float32
    finish = wide <= 128
    flat = plane_of(n, m)
    gram = (n, PAD, wide)
    cent = (n, PAD, width)
    if finish:
        shapes = [(1, rows), prev_update.shape]
        scratch = [pltpu.VMEM(cent, f32)]
    else:
        shapes = [(rows, 128), gram, cent]
        scratch = []
    return pl.pallas_call(
        functools.partial(step_kernel, n, m, finish),
        out_shape=[jax.ShapeDtypeStruct(shape, f32) for shape in shapes],
        in_specs=[vmem] * 3,
        out_specs=[vmem] * len(shapes),
        scratch_shapes=scratch
        + [
            pltpu.VMEM(gram, f32),
            pltpu.VMEM((flat * m, n // (flat * m), PAD, wide), f32),
            pltpu.VMEM((n // flat, n // (flat * m), PAD, wide), f32),
            pltpu.VMEM(gram, f32),
        ]
        + [pltpu.SemaphoreType.DMA] * 6,
        compiler_params=pltpu.CompilerParams(
            collective_id=0, has_side_effects=True, vmem_limit_bytes=32 * 1024 * 1024
        ),
    )(cols, energies, prev_update)


def finish_outside(n, rows, gram, cent, prev_update):
    walkers = n * rows
    along = gram[:, :rows, rows].reshape(walkers)
    energies = gram[:, :rows, rows + 1].reshape(walkers)
    square = gram.reshape(n, PAD, n, PAD)[:, :rows, :, :rows].reshape(walkers, walkers)
    eps = -(energies - jnp.mean(energies)) / math.sqrt(walkers)
    system = square + damping * jnp.eye(walkers, dtype=jnp.float32)
    factor = jnp.linalg.cholesky(system)
    solved = jax.scipy.linalg.cho_solve((factor, True), eps - momentum * along)
    flat = cent[:, :rows, :].reshape(walkers, -1)
    update = jnp.dot(
        solved, flat, precision=lax.Precision.HIGHEST, preferred_element_type=jnp.float32
    )
    return update[None, :] + momentum * prev_update


def body(
    n,
    m,
    jacobian,
    prev_update,
    base_energy,
    elec_pos,
    atom_pos,
    quad_ratio,
    rotation,
    channels,
    ecp_coef,
    ecp_expo,
):
    rows = jacobian.shape[0]
    split = jacobian.reshape(rows, n, -1)
    cols = lax.all_to_all(split, "walk", split_axis=1, concat_axis=0, tiled=False)
    energies = walkers_mine(
        m,
        elec_pos,
        atom_pos,
        jnp.transpose(quad_ratio, (0, 3, 1, 2)),
        rotation,
        channels.reshape(1, -1),
        ecp_coef.T,
        ecp_expo.T,
        base_energy.reshape(1, -1),
    )
    energy, result, *cent = step(n, m, cols, energies, prev_update)
    if cent:
        return (energy[:, 0], finish_outside(n, rows, result, cent[0], prev_update))
    return (energy.reshape(rows), result)


def solution(mesh):
    in_specs = (
        P("walk", "col"),
        P("col", "walk"),
        P("walk"),
        P("walk", None, None),
        P(),
        P("walk", None, None, None),
        P("walk", None),
        P(),
        P(),
        P(),
    )
    out_specs = (P("walk"), P("col", "walk"))
    run = functools.partial(body, mesh.shape["walk"], mesh.shape["col"])
    return jax.shard_map(run, mesh=mesh, in_specs=in_specs, out_specs=out_specs, check_vma=False)
```

```python
import functools
import math

import jax
import jax.numpy as jnp
from jax import lax
from jax.experimental import pallas as pl
from jax.experimental.pallas import tpu as pltpu
from jax.sharding import PartitionSpec as P

NROT = 16


momentum = 0.9
damping = 0.1


MESH = pl.DeviceIdType.MESH
PAD = 8
CHUNKS = 2


def icosa_points():
    golden = (1.0 + math.sqrt(5.0)) / 2.0
    length = math.sqrt(1.0 + golden * golden)
    rows = []
    for first in (-1.0, 1.0):
        for second in (-golden, golden):
            rows.append((0.0, first / length, second / length))
            rows.append((first / length, second / length, 0.0))
            rows.append((second / length, 0.0, first / length))
    return rows


def rotation_table(count):
    points = icosa_points()
    quad = len(points)
    angle = lax.broadcasted_iota(jnp.int32, (1, count), 1).astype(jnp.float32)
    turn_z = 2.0 * math.pi * angle / count
    turn_x = 0.9 * angle
    cz, sz = (jnp.cos(turn_z), jnp.sin(turn_z))
    cx, sx = (jnp.cos(turn_x), jnp.sin(turn_x))
    matrix = [[cz, -sz * cx, sz * sx], [sz, cz * cx, -cz * sx], [jnp.zeros_like(cz), sx, cx]]
    index = lax.broadcasted_iota(jnp.int32, (quad, count), 0)
    place = []
    for d in range(3):
        column = jnp.zeros((quad, count), jnp.float32)
        for j in range(quad):
            column = jnp.where(index == j, points[j][d], column)
        place.append(column)
    return [
        matrix[c][0] * place[0] + matrix[c][1] * place[1] + matrix[c][2] * place[2]
        for c in range(3)
    ]


def as_column(row):
    count = row.shape[1]
    index = lax.broadcasted_iota(jnp.int32, (count, count), 0)
    other = lax.broadcasted_iota(jnp.int32, (count, count), 1)
    return jnp.sum(jnp.where(index == other, row, 0.0), axis=1, keepdims=True)


def walker_energies(share, begin, elec, atom, quad, rotation, channels, coef, expo, base, out):
    rows, points, atoms, electrons = quad.shape
    lmax = coef.shape[0]
    table = rotation_table(NROT)
    spot = [as_column(atom[c : c + 1, :]) for c in range(3)]
    count = as_column(channels[...].astype(jnp.float32))
    strength = [as_column(coef[level : level + 1, :]) for level in range(lmax)]
    decay = [as_column(expo[level : level + 1, :]) for level in range(lmax)]
    first = as_column(base[...])
    out[...] = jnp.zeros_like(out)
    kind = lax.broadcasted_iota(jnp.int32, (NROT, electrons), 0)

    def walker(k, _):
        w = lax.rem(begin + k, rows)
        onehot = (kind == rotation[pl.ds(w, 1), :]).astype(jnp.float32)
        turned = [
            jnp.dot(
                table[c], onehot, precision=lax.Precision.HIGHEST, preferred_element_type=jnp.float32
            )
            for c in range(3)
        ]
        where = elec[w]
        diff = [where[c : c + 1, :] - spot[c] for c in range(3)]
        dist2 = diff[0] * diff[0] + diff[1] * diff[1] + diff[2] * diff[2]
        root = jnp.sqrt(dist2 + 0.01)
        unit = [d / root for d in diff]
        angular = [jnp.zeros((atoms, electrons), jnp.float32) for _ in range(lmax)]
        for j in range(points):
            ratio = quad[w, j]
            cosang = unit[0] * turned[0][j : j + 1, :]
            cosang = cosang + unit[1] * turned[1][j : j + 1, :]
            cosang = cosang + unit[2] * turned[2][j : j + 1, :]
            lower, upper = None, None
            for level in range(lmax):
                if level == 0:
                    angular[0] = angular[0] + ratio
                    continue
                if level == 1:
                    lower, upper = 1.0, cosang
                else:
                    fresh = ((2 * level - 1) * cosang * upper - (level - 1) * lower) * (1.0 / level)
                    lower, upper = upper, fresh
                angular[level] = angular[level] + upper * ratio
        total = jnp.zeros((atoms, electrons), jnp.float32)
        for level in range(lmax):
            active = (count > level).astype(jnp.float32)
            radial = (strength[level] * active) * jnp.exp(-decay[level] * dist2)
            total = total + ((2 * level + 1) / points) * radial * angular[level]
        value = jnp.sum(jnp.sum(total, axis=1, keepdims=True), axis=0, keepdims=True)
        out[pl.ds(w, 1), :] = jnp.broadcast_to(value, (1, out.shape[1]))
        return 0

    lax.fori_loop(0, share, walker, 0)
    place = lax.broadcasted_iota(jnp.int32, (rows, out.shape[1]), 0)
    mine = (place >= begin) & (place < begin + share)
    out[0:rows, :] = jnp.where(mine, out[0:rows, :] + first, 0.0)


def far_first(n):
    order, span = [], n
    while span > 1:
        order += [s for s in range(span // 2, n, span)]
        span //= 2
    return order + [s for s in range(1, n) if s not in order]


def each(count, act):
    if count <= 64:
        for s in far_first(count):
            act(s)
        return

    def turn(s, _):
        act(s)
        return 0

    lax.fori_loop(1, count, turn, 0)


def spread_energy(full, me, rows):
    return jnp.broadcast_to(full[me][0:rows, rows + 1 : rows + 2], (rows, 128))


def step_kernel(
    n,
    m,
    finish,
    jac_ref,
    prev_ref,
    base_ref,
    elec_ref,
    atom_ref,
    quad_ref,
    rotation_ref,
    channels_ref,
    coef_ref,
    expo_ref,
    energy_ref,
    result_ref,
    cent_ref,
    prev,
    base,
    elec,
    atom,
    quad,
    rotation,
    channels,
    coef,
    expo,
    cols,
    part,
    shares,
    full,
    energies,
    fetch_sem,
    jac_send,
    jac_recv,
    rs_send,
    rs_recv,
    ag_send,
    ag_recv,
):
    me = lax.axis_index("walk")
    my_col = lax.axis_index("col")
    chunks, _, rows, span = cols.shape
    width = chunks * span
    walkers = rows * n
    scale = 1.0 / (width * n * m)
    order = far_first(n)
    barrier = pltpu.get_barrier_semaphore()
    mine = me * m + my_col
    owner = lax.rem(me, m) == my_col

    def device(s):
        place = lax.rem(mine + s, n * m)
        return place // m, lax.rem(place, m)

    def greet(s):
        pl.semaphore_signal(barrier, inc=1, device_id=device(s), device_id_type=MESH)

    each(n * m, greet)
    sources = (
        quad_ref,
        prev_ref,
        base_ref,
        elec_ref,
        atom_ref,
        rotation_ref,
        channels_ref,
        coef_ref,
        expo_ref,
    )
    targets = (quad, prev, base, elec, atom, rotation, channels, coef, expo)
    fetches = [
        pltpu.make_async_copy(source, target, fetch_sem.at[k])
        for k, (source, target) in enumerate(zip(sources, targets))
    ]
    for fetch in fetches:
        fetch.start()
    pl.semaphore_wait(barrier, n * m - 1)

    def block(index, k):
        return jac_ref.at[:, pl.ds(pl.multiple_of(index * width + k * span, span), span)]

    def send(src, dst, send_sem, recv_sem, s):
        pltpu.make_async_remote_copy(
            src_ref=src,
            dst_ref=dst.at[me],
            send_sem=send_sem,
            recv_sem=recv_sem,
            device_id=(lax.rem(me + s, n), my_col),
            device_id_type=MESH,
        ).start()

    def wait_bytes(like, sem):
        pltpu.make_async_copy(like, like, sem).wait()

    for k in range(chunks):
        for s in order:
            send(block(lax.rem(me + s, n), k), cols.at[k], jac_send.at[k], jac_recv.at[k], s)
        pltpu.make_async_copy(block(me, k), cols.at[k, me], jac_recv.at[k]).start()

    for fetch in fetches:
        fetch.wait()
    share = -(-rows // m)
    walker_energies(share, my_col * share, elec, atom, quad, rotation, channels, coef, expo, base, energies)
    cent_ref[...] = jnp.zeros_like(cent_ref)
    cent_ref[0, rows : rows + 1, :] = prev[...]

    gram = None
    for k in range(chunks):
        wait_bytes(cols.at[k], jac_recv.at[k])
        total = cols[k, 0]
        for i in range(1, n):
            total = total + cols[k, i]
        mean = jnp.sum(total, axis=0, keepdims=True) * (1.0 / walkers)
        for i in range(n):
            cent_ref[i, 0:rows, k * span : (k + 1) * span] = cols[k, i] - mean
        cent = cent_ref[:, :, k * span : (k + 1) * span].reshape(n * PAD, span)
        piece = lax.dot_general(
            cent,
            cent,
            (((1,), (1,)), ((), ())),
            precision=lax.Precision.HIGHEST,
            preferred_element_type=jnp.float32,
        )
        gram = piece if gram is None else gram + piece
    part[...] = (gram * scale).reshape(part.shape)
    lane = lax.broadcasted_iota(jnp.int32, part.shape[1:], 1)
    spare = jnp.broadcast_to(energies[:, 0:1], part.shape[1:])
    part[me] = jnp.where(lane == rows + 1, spare, part[me])

    def send_part(there):
        pltpu.make_async_remote_copy(
            src_ref=part.at[there],
            dst_ref=shares.at[mine],
            send_sem=rs_send,
            recv_sem=rs_recv,
            device_id=(there, lax.rem(there, m)),
            device_id_type=MESH,
        ).start()

    def send_sum(s):
        pltpu.make_async_remote_copy(
            src_ref=full.at[me],
            dst_ref=full.at[me],
            send_sem=ag_send,
            recv_sem=ag_recv,
            device_id=device(s),
            device_id_type=MESH,
        ).start()

    for s in order:
        send_part(lax.rem(me + s, n))

    @pl.when(jnp.logical_not(owner))
    def _():
        send_part(me)
        wait_bytes(full, ag_recv)
        wait_bytes(part, rs_send)

    @pl.when(owner)
    def _():
        shares[mine] = part[me]
        wait_bytes(shares.at[pl.ds(0, n * m - 1)], rs_recv)
        sums = [shares[i] for i in range(n * m)]
        while len(sums) > 1:
            sums = [sum(sums[i : i + 2]) for i in range(0, len(sums), 2)]
        full[me] = sums[0]
        each(n * m, send_sum)
        wait_bytes(full.at[pl.ds(0, n - 1)], ag_recv)
        wait_bytes(part.at[pl.ds(0, n - 1)], rs_send)

    if finish:
        solve(n, rows, full, cent_ref, prev, spread_energy(full, me, rows), result_ref, energy_ref)
    else:
        result_ref[...] = full[...]
        energy_ref[...] = spread_energy(full, me, rows)

    for k in range(chunks):
        wait_bytes(cols.at[k, pl.ds(0, n - 1)], jac_send.at[k])
    @pl.when(owner)
    def _():
        wait_bytes(shares.at[pl.ds(0, n * m - 1)], ag_send)


def solve(n, rows, gram_ref, cent_ref, prev_ref, energy_ref, out_ref, mine_ref):
    index = lax.broadcasted_iota(jnp.int32, (rows, rows), 0)
    other = lax.broadcasted_iota(jnp.int32, (rows, rows), 1)
    mine_ref[...] = jnp.sum(
        jnp.where(index == other, energy_ref[:, 0:rows], 0.0), axis=0, keepdims=True
    )
    wide = n * PAD
    walkers = n * rows
    sub = lax.broadcasted_iota(jnp.int32, (PAD, wide), 0)
    lane = lax.broadcasted_iota(jnp.int32, (PAD, wide), 1)
    real_row = sub < rows
    real = real_row & (lane % PAD < rows)
    energies = [
        jnp.broadcast_to(gram_ref[i][:, rows + 1 : rows + 2], (PAD, wide)) for i in range(n)
    ]
    esum = energies[0]
    for i in range(1, n):
        esum = esum + energies[i]
    emean = jnp.sum(jnp.where(real_row, esum, 0.0), axis=0, keepdims=True) * (1.0 / walkers)
    panels = []
    for i in range(n):
        g = gram_ref[i]
        eps = -(energies[i] - emean) * (1.0 / math.sqrt(walkers))
        along = jnp.broadcast_to(g[:, rows : rows + 1], (PAD, wide))
        right = eps - momentum * along
        panel = jnp.where(real, g, 0.0)
        panel = jnp.where(real & (lane == sub + i * PAD), panel + damping, panel)
        panels.append(jnp.where(real_row & (lane == rows), right, panel))

    def spread(panel, column):
        return jnp.broadcast_to(panel[:, column : column + 1], (PAD, wide))

    for g in range(n):
        top = panels[g]
        marks = [spread(top, g * PAD + r) for r in range(rows)]
        for r in range(rows):
            inverse = 1.0 / marks[r][r : r + 1, :]
            here = sub == r
            factor = jnp.where(here, 0.0, marks[r])
            line = top[r : r + 1, :] * inverse
            top = jnp.where(here, line, top - factor * line)
            for q in range(r + 1, rows):
                line_q = marks[q][r : r + 1, :] * inverse
                marks[q] = jnp.where(here, line_q, marks[q] - factor * line_q)
        for i in range(n):
            if i == g:
                continue
            panel = panels[i]
            fresh = panel
            for r in range(rows):
                fresh = fresh - spread(panel, g * PAD + r) * top[r : r + 1, :]
            panels[i] = fresh
        panels[g] = top

    width = cent_ref.shape[2]
    acc = jnp.zeros((PAD, width), jnp.float32)
    keep = lax.broadcasted_iota(jnp.int32, (PAD, width), 0) < rows
    for i in range(n):
        solved = jnp.broadcast_to(panels[i][:, rows : rows + 1], (PAD, width))
        acc = acc + solved * cent_ref[i]
    acc = jnp.where(keep, acc, 0.0)
    out_ref[...] = jnp.sum(acc, axis=0, keepdims=True) + momentum * prev_ref[...]


def step(n, m, jacobian, prev_update, base, elec_pos, atom_pos, quad, rotation, channels, coef, expo):
    rows = jacobian.shape[0]
    width = jacobian.shape[1] // n
    wide = n * PAD
    vmem = pl.BlockSpec(memory_space=pltpu.VMEM)
    hbm = pl.BlockSpec(memory_space=pltpu.HBM)
    f32 = jnp.float32
    dma = pltpu.SemaphoreType.DMA
    small = (prev_update, base, elec_pos, atom_pos, quad, rotation, channels, coef, expo)
    finish = wide <= 128
    gram = (n, PAD, wide)
    cent = (n, PAD, width)
    scratch = [pltpu.VMEM(x.shape, x.dtype) for x in small]
    if finish:
        shapes = [(1, rows), prev_update.shape]
        scratch = [pltpu.VMEM(cent, f32)] + scratch
    else:
        shapes = [(rows, 128), gram, cent]
    return pl.pallas_call(
        functools.partial(step_kernel, n, m, finish),
        out_shape=[jax.ShapeDtypeStruct(shape, f32) for shape in shapes],
        in_specs=[hbm] * 10,
        out_specs=[vmem] * len(shapes),
        scratch_shapes=scratch
        + [
            pltpu.VMEM((CHUNKS, n, rows, width // CHUNKS), f32),
            pltpu.VMEM(gram, f32),
            pltpu.VMEM((n * m, PAD, wide), f32),
            pltpu.VMEM(gram, f32),
            pltpu.VMEM((PAD, 128), f32),
        ]
        + [dma((len(small),)), dma((CHUNKS,)), dma((CHUNKS,))]
        + [dma] * 4,
        compiler_params=pltpu.CompilerParams(collective_id=0, has_side_effects=True, vmem_limit_bytes=60 * 1024 * 1024),
    )(jacobian, *small)


def finish_outside(n, rows, gram, cent, prev_update):
    walkers = n * rows
    along = gram[:, :rows, rows].reshape(walkers)
    energies = gram[:, :rows, rows + 1].reshape(walkers)
    square = gram.reshape(n, PAD, n, PAD)[:, :rows, :, :rows].reshape(walkers, walkers)
    eps = -(energies - jnp.mean(energies)) / math.sqrt(walkers)
    system = square + damping * jnp.eye(walkers, dtype=jnp.float32)
    factor = jnp.linalg.cholesky(system)
    solved = jax.scipy.linalg.cho_solve((factor, True), eps - momentum * along)
    flat = cent[:, :rows, :].reshape(walkers, -1)
    update = jnp.dot(
        solved, flat, precision=lax.Precision.HIGHEST, preferred_element_type=jnp.float32
    )
    return update[None, :] + momentum * prev_update


def body(
    n,
    m,
    jacobian,
    prev_update,
    base_energy,
    elec_pos,
    atom_pos,
    quad_ratio,
    rotation,
    channels,
    ecp_coef,
    ecp_expo,
):
    rows = jacobian.shape[0]
    energy, result, *cent = step(
        n,
        m,
        jacobian,
        prev_update,
        base_energy.reshape(1, -1),
        elec_pos,
        atom_pos,
        jnp.transpose(quad_ratio, (0, 3, 1, 2)),
        rotation,
        channels.reshape(1, -1),
        ecp_coef.T,
        ecp_expo.T,
    )
    if cent:
        return (energy[:, 0], finish_outside(n, rows, result, cent[0], prev_update))
    return (energy.reshape(rows), result)


def solution(mesh):
    in_specs = (
        P("walk", "col"),
        P("col", "walk"),
        P("walk"),
        P("walk", None, None),
        P(),
        P("walk", None, None, None),
        P("walk", None),
        P(),
        P(),
        P(),
    )
    out_specs = (P("walk"), P("col", "walk"))
    run = functools.partial(body, mesh.shape["walk"], mesh.shape["col"])
    return jax.shard_map(run, mesh=mesh, in_specs=in_specs, out_specs=out_specs, check_vma=False)
```

```python
import functools
import math

import jax
import jax.numpy as jnp
from jax import lax
from jax.experimental import pallas as pl
from jax.experimental.pallas import tpu as pltpu
from jax.sharding import PartitionSpec as P

NROT = 16


momentum = 0.9
damping = 0.1


MESH = pl.DeviceIdType.MESH
PAD = 8
CHUNKS = 1


def icosa_points():
    golden = (1.0 + math.sqrt(5.0)) / 2.0
    length = math.sqrt(1.0 + golden * golden)
    rows = []
    for first in (-1.0, 1.0):
        for second in (-golden, golden):
            rows.append((0.0, first / length, second / length))
            rows.append((first / length, second / length, 0.0))
            rows.append((second / length, 0.0, first / length))
    return rows


def rotation_table(count):
    points = icosa_points()
    quad = len(points)
    angle = lax.broadcasted_iota(jnp.int32, (1, count), 1).astype(jnp.float32)
    turn_z = 2.0 * math.pi * angle / count
    turn_x = 0.9 * angle
    cz, sz = (jnp.cos(turn_z), jnp.sin(turn_z))
    cx, sx = (jnp.cos(turn_x), jnp.sin(turn_x))
    matrix = [[cz, -sz * cx, sz * sx], [sz, cz * cx, -cz * sx], [jnp.zeros_like(cz), sx, cx]]
    index = lax.broadcasted_iota(jnp.int32, (quad, count), 0)
    place = []
    for d in range(3):
        column = jnp.zeros((quad, count), jnp.float32)
        for j in range(quad):
            column = jnp.where(index == j, points[j][d], column)
        place.append(column)
    return [
        matrix[c][0] * place[0] + matrix[c][1] * place[1] + matrix[c][2] * place[2]
        for c in range(3)
    ]


def as_column(row):
    count = row.shape[1]
    index = lax.broadcasted_iota(jnp.int32, (count, count), 0)
    other = lax.broadcasted_iota(jnp.int32, (count, count), 1)
    return jnp.sum(jnp.where(index == other, row, 0.0), axis=1, keepdims=True)


def walker_energies(elec, atom, quad, rotation, channels, coef, expo, base, out):
    rows, points, atoms, electrons = quad.shape
    lmax = coef.shape[0]
    table = rotation_table(NROT)
    spot = [as_column(atom[c : c + 1, :]) for c in range(3)]
    count = as_column(channels[...].astype(jnp.float32))
    strength = [as_column(coef[level : level + 1, :]) for level in range(lmax)]
    decay = [as_column(expo[level : level + 1, :]) for level in range(lmax)]
    first = as_column(base[...])
    out[...] = jnp.zeros_like(out)
    kind = lax.broadcasted_iota(jnp.int32, (NROT, electrons), 0)

    def walker(w, _):
        onehot = (kind == rotation[pl.ds(w, 1), :]).astype(jnp.float32)
        turned = [
            jnp.dot(
                table[c], onehot, precision=lax.Precision.HIGHEST, preferred_element_type=jnp.float32
            )
            for c in range(3)
        ]
        where = elec[w]
        diff = [where[c : c + 1, :] - spot[c] for c in range(3)]
        dist2 = diff[0] * diff[0] + diff[1] * diff[1] + diff[2] * diff[2]
        root = jnp.sqrt(dist2 + 0.01)
        unit = [d / root for d in diff]
        angular = [jnp.zeros((atoms, electrons), jnp.float32) for _ in range(lmax)]
        for j in range(points):
            ratio = quad[w, j]
            cosang = unit[0] * turned[0][j : j + 1, :]
            cosang = cosang + unit[1] * turned[1][j : j + 1, :]
            cosang = cosang + unit[2] * turned[2][j : j + 1, :]
            lower, upper = None, None
            for level in range(lmax):
                if level == 0:
                    angular[0] = angular[0] + ratio
                    continue
                if level == 1:
                    lower, upper = 1.0, cosang
                else:
                    fresh = ((2 * level - 1) * cosang * upper - (level - 1) * lower) * (1.0 / level)
                    lower, upper = upper, fresh
                angular[level] = angular[level] + upper * ratio
        total = jnp.zeros((atoms, electrons), jnp.float32)
        for level in range(lmax):
            active = (count > level).astype(jnp.float32)
            radial = (strength[level] * active) * jnp.exp(-decay[level] * dist2)
            total = total + ((2 * level + 1) / points) * radial * angular[level]
        value = jnp.sum(jnp.sum(total, axis=1, keepdims=True), axis=0, keepdims=True)
        out[pl.ds(w, 1), :] = jnp.broadcast_to(value, (1, out.shape[1]))
        return 0

    lax.fori_loop(0, rows, walker, 0)
    out[0:rows, :] = out[0:rows, :] + first


def far_first(n):
    order, span = [], n
    while span > 1:
        order += [s for s in range(span // 2, n, span)]
        span //= 2
    return order + [s for s in range(1, n) if s not in order]


def step_kernel(
    n,
    m,
    finish,
    jac_ref,
    prev_ref,
    base_ref,
    elec_ref,
    atom_ref,
    quad_ref,
    rotation_ref,
    channels_ref,
    coef_ref,
    expo_ref,
    energy_ref,
    result_ref,
    cent_ref,
    prev,
    base,
    elec,
    atom,
    quad,
    rotation,
    channels,
    coef,
    expo,
    cols,
    relay,
    part,
    shares,
    pair,
    full,
    energies,
    fetch_sem,
    line_send,
    line_recv,
    jac_send,
    jac_recv,
    rs_send,
    rs_recv,
    pair_send,
    pair_recv,
    ag_send,
    ag_recv,
):
    me = lax.axis_index("walk")
    my_col = lax.axis_index("col")
    chunks, _, rows, span = cols.shape
    width = chunks * span
    walkers = rows * n
    scale = 1.0 / (width * n * m)
    order = far_first(n)
    layers = relay.shape[0]
    flat = n // layers
    layer = me // flat
    inner = lax.rem(me, flat)
    barrier = pltpu.get_barrier_semaphore()
    for s in order:
        pl.semaphore_signal(
            barrier, inc=1, device_id=(lax.rem(me + s, n), my_col), device_id_type=MESH
        )
    for s in range(1, m):
        pl.semaphore_signal(
            barrier, inc=1, device_id=(me, lax.rem(my_col + s, m)), device_id_type=MESH
        )
    sources = (
        quad_ref,
        prev_ref,
        base_ref,
        elec_ref,
        atom_ref,
        rotation_ref,
        channels_ref,
        coef_ref,
        expo_ref,
    )
    targets = (quad, prev, base, elec, atom, rotation, channels, coef, expo)
    fetches = [
        pltpu.make_async_copy(source, target, fetch_sem.at[k])
        for k, (source, target) in enumerate(zip(sources, targets))
    ]
    for fetch in fetches:
        fetch.start()
    pl.semaphore_wait(barrier, n + m - 2)

    def block(index, k):
        return jac_ref.at[:, pl.ds(pl.multiple_of(index * width + k * span, span), span)]

    def send(src, dst, send_sem, recv_sem, s):
        pltpu.make_async_remote_copy(
            src_ref=src,
            dst_ref=dst.at[me],
            send_sem=send_sem,
            recv_sem=recv_sem,
            device_id=(lax.rem(me + s, n), my_col),
            device_id_type=MESH,
        ).start()

    def wait_bytes(like, sem):
        pltpu.make_async_copy(like, like, sem).wait()

    for s in far_first(layers):
        there = lax.rem(layer + s, layers)
        bulk = flat * width
        pltpu.make_async_remote_copy(
            src_ref=jac_ref.at[:, pl.ds(pl.multiple_of(there * bulk, bulk), bulk)],
            dst_ref=relay.at[layer],
            send_sem=line_send,
            recv_sem=line_recv.at[layer],
            device_id=(there * flat + inner, my_col),
            device_id_type=MESH,
        ).start()

    def hand_out(pick, origin):
        for s in range(1, flat):
            there = lax.rem(inner + s, flat)
            pltpu.make_async_remote_copy(
                src_ref=pick(there),
                dst_ref=cols.at[0, origin],
                send_sem=jac_send.at[0],
                recv_sem=jac_recv.at[0],
                device_id=(layer * flat + there, my_col),
                device_id_type=MESH,
            ).start()
        pltpu.make_async_copy(pick(inner), cols.at[0, origin], jac_recv.at[0]).start()

    hand_out(lambda there: block(layer * flat + there, 0), me)

    for fetch in fetches:
        fetch.wait()
    walker_energies(elec, atom, quad, rotation, channels, coef, expo, base, energies)
    for s in far_first(layers):
        origin = lax.rem(layer + layers - s, layers)
        wait_bytes(relay.at[origin], line_recv.at[origin])

        def pick(there):
            return relay.at[origin, :, pl.ds(pl.multiple_of(there * width, width), width)]

        hand_out(pick, origin * flat + inner)
    cent_ref[...] = jnp.zeros_like(cent_ref)
    cent_ref[0, rows : rows + 1, :] = prev[...]

    gram = None
    for k in range(chunks):
        wait_bytes(cols.at[k], jac_recv.at[k])
        total = cols[k, 0]
        for i in range(1, n):
            total = total + cols[k, i]
        mean = jnp.sum(total, axis=0, keepdims=True) * (1.0 / walkers)
        for i in range(n):
            cent_ref[i, 0:rows, k * span : (k + 1) * span] = cols[k, i] - mean
        cent = cent_ref[:, :, k * span : (k + 1) * span].reshape(n * PAD, span)
        piece = lax.dot_general(
            cent,
            cent,
            (((1,), (1,)), ((), ())),
            precision=lax.Precision.HIGHEST,
            preferred_element_type=jnp.float32,
        )
        gram = piece if gram is None else gram + piece
    part[...] = gram.reshape(part.shape)

    for s in order:
        send(part.at[lax.rem(me + s, n)], shares, rs_send, rs_recv, s)
    shares[me] = part[me]
    wait_bytes(shares.at[pl.ds(0, n - 1)], rs_recv)
    acc = shares[0]
    for i in range(1, n):
        acc = acc + shares[i]
    pair[my_col] = acc

    def pair_copy(s, origin):
        return pltpu.make_async_remote_copy(
            src_ref=pair.at[my_col],
            dst_ref=pair.at[origin],
            send_sem=pair_send.at[s],
            recv_sem=pair_recv.at[origin],
            device_id=(me, lax.rem(my_col + s, m)),
            device_id_type=MESH,
        )

    for s in range(1, m):
        pair_copy(s, my_col).start()
    for s in range(1, m):
        pair_copy(s, lax.rem(my_col + s, m)).wait_recv()
    acc = pair[0]
    for c in range(1, m):
        acc = acc + pair[c]
    lane = lax.broadcasted_iota(jnp.int32, acc.shape, 1)
    spare = jnp.broadcast_to(energies[:, 0:1], acc.shape)
    full[me] = jnp.where(lane == rows + 1, spare, acc * scale)

    for s in order:
        send(full.at[me], full, ag_send, ag_recv, s)
    wait_bytes(full.at[pl.ds(0, n - 1)], ag_recv)
    if finish:
        solve(n, rows, full, cent_ref, prev, energies, result_ref, energy_ref)
    else:
        result_ref[...] = full[...]
        energy_ref[...] = jnp.broadcast_to(energies[0:rows, 0:1], (rows, 128))

    for k in range(chunks):
        wait_bytes(cols.at[k, pl.ds(0, n - layers)], jac_send.at[k])
    wait_bytes(relay.at[pl.ds(0, layers - 1)], line_send)
    wait_bytes(part.at[pl.ds(0, n - 1)], rs_send)
    wait_bytes(full.at[pl.ds(0, n - 1)], ag_send)
    for s in range(1, m):
        pair_copy(s, my_col).wait_send()


def solve(n, rows, gram_ref, cent_ref, prev_ref, energy_ref, out_ref, mine_ref):
    index = lax.broadcasted_iota(jnp.int32, (rows, rows), 0)
    other = lax.broadcasted_iota(jnp.int32, (rows, rows), 1)
    mine_ref[...] = jnp.sum(
        jnp.where(index == other, energy_ref[0:rows, 0:rows], 0.0), axis=0, keepdims=True
    )
    wide = n * PAD
    walkers = n * rows
    sub = lax.broadcasted_iota(jnp.int32, (PAD, wide), 0)
    lane = lax.broadcasted_iota(jnp.int32, (PAD, wide), 1)
    real_row = sub < rows
    real = real_row & (lane % PAD < rows)
    energies = [
        jnp.broadcast_to(gram_ref[i][:, rows + 1 : rows + 2], (PAD, wide)) for i in range(n)
    ]
    esum = energies[0]
    for i in range(1, n):
        esum = esum + energies[i]
    emean = jnp.sum(jnp.where(real_row, esum, 0.0), axis=0, keepdims=True) * (1.0 / walkers)
    panels = []
    for i in range(n):
        g = gram_ref[i]
        eps = -(energies[i] - emean) * (1.0 / math.sqrt(walkers))
        along = jnp.broadcast_to(g[:, rows : rows + 1], (PAD, wide))
        right = eps - momentum * along
        panel = jnp.where(real, g, 0.0)
        panel = jnp.where(real & (lane == sub + i * PAD), panel + damping, panel)
        panels.append(jnp.where(real_row & (lane == rows), right, panel))

    def spread(panel, column):
        return jnp.broadcast_to(panel[:, column : column + 1], (PAD, wide))

    for g in range(n):
        top = panels[g]
        marks = [spread(top, g * PAD + r) for r in range(rows)]
        for r in range(rows):
            inverse = 1.0 / marks[r][r : r + 1, :]
            here = sub == r
            factor = jnp.where(here, 0.0, marks[r])
            line = top[r : r + 1, :] * inverse
            top = jnp.where(here, line, top - factor * line)
            for q in range(r + 1, rows):
                line_q = marks[q][r : r + 1, :] * inverse
                marks[q] = jnp.where(here, line_q, marks[q] - factor * line_q)
        for i in range(n):
            if i == g:
                continue
            panel = panels[i]
            fresh = panel
            for r in range(rows):
                fresh = fresh - spread(panel, g * PAD + r) * top[r : r + 1, :]
            panels[i] = fresh
        panels[g] = top

    width = cent_ref.shape[2]
    acc = jnp.zeros((PAD, width), jnp.float32)
    keep = lax.broadcasted_iota(jnp.int32, (PAD, width), 0) < rows
    for i in range(n):
        solved = jnp.broadcast_to(panels[i][:, rows : rows + 1], (PAD, width))
        acc = acc + solved * cent_ref[i]
    acc = jnp.where(keep, acc, 0.0)
    out_ref[...] = jnp.sum(acc, axis=0, keepdims=True) + momentum * prev_ref[...]


def step(n, m, jacobian, prev_update, base, elec_pos, atom_pos, quad, rotation, channels, coef, expo):
    rows = jacobian.shape[0]
    width = jacobian.shape[1] // n
    wide = n * PAD
    vmem = pl.BlockSpec(memory_space=pltpu.VMEM)
    hbm = pl.BlockSpec(memory_space=pltpu.HBM)
    f32 = jnp.float32
    dma = pltpu.SemaphoreType.DMA
    small = (prev_update, base, elec_pos, atom_pos, quad, rotation, channels, coef, expo)
    finish = wide <= 128
    flat = 4 if n % 4 == 0 else 1
    gram = (n, PAD, wide)
    cent = (n, PAD, width)
    scratch = [pltpu.VMEM(x.shape, x.dtype) for x in small]
    if finish:
        shapes = [(1, rows), prev_update.shape]
        scratch = [pltpu.VMEM(cent, f32)] + scratch
    else:
        shapes = [(rows, 128), gram, cent]
    return pl.pallas_call(
        functools.partial(step_kernel, n, m, finish),
        out_shape=[jax.ShapeDtypeStruct(shape, f32) for shape in shapes],
        in_specs=[hbm] * 10,
        out_specs=[vmem] * len(shapes),
        scratch_shapes=scratch
        + [
            pltpu.VMEM((CHUNKS, n, rows, width // CHUNKS), f32),
            pltpu.VMEM((n // flat, rows, flat * width), f32),
            pltpu.VMEM(gram, f32),
            pltpu.VMEM(gram, f32),
            pltpu.VMEM((m, PAD, wide), f32),
            pltpu.VMEM(gram, f32),
            pltpu.VMEM((PAD, 128), f32),
        ]
        + [dma((len(small),)), dma, dma((n // flat,)), dma((CHUNKS,)), dma((CHUNKS,)), dma, dma]
        + [dma((m,))] * 2
        + [dma] * 2,
        compiler_params=pltpu.CompilerParams(collective_id=0, has_side_effects=True, vmem_limit_bytes=60 * 1024 * 1024),
    )(jacobian, *small)


def finish_outside(n, rows, gram, cent, prev_update):
    walkers = n * rows
    along = gram[:, :rows, rows].reshape(walkers)
    energies = gram[:, :rows, rows + 1].reshape(walkers)
    square = gram.reshape(n, PAD, n, PAD)[:, :rows, :, :rows].reshape(walkers, walkers)
    eps = -(energies - jnp.mean(energies)) / math.sqrt(walkers)
    system = square + damping * jnp.eye(walkers, dtype=jnp.float32)
    factor = jnp.linalg.cholesky(system)
    solved = jax.scipy.linalg.cho_solve((factor, True), eps - momentum * along)
    flat = cent[:, :rows, :].reshape(walkers, -1)
    update = jnp.dot(
        solved, flat, precision=lax.Precision.HIGHEST, preferred_element_type=jnp.float32
    )
    return update[None, :] + momentum * prev_update


def body(
    n,
    m,
    jacobian,
    prev_update,
    base_energy,
    elec_pos,
    atom_pos,
    quad_ratio,
    rotation,
    channels,
    ecp_coef,
    ecp_expo,
):
    rows = jacobian.shape[0]
    energy, result, *cent = step(
        n,
        m,
        jacobian,
        prev_update,
        base_energy.reshape(1, -1),
        elec_pos,
        atom_pos,
        jnp.transpose(quad_ratio, (0, 3, 1, 2)),
        rotation,
        channels.reshape(1, -1),
        ecp_coef.T,
        ecp_expo.T,
    )
    if cent:
        return (energy[:, 0], finish_outside(n, rows, result, cent[0], prev_update))
    return (energy.reshape(rows), result)


def solution(mesh):
    in_specs = (
        P("walk", "col"),
        P("col", "walk"),
        P("walk"),
        P("walk", None, None),
        P(),
        P("walk", None, None, None),
        P("walk", None),
        P(),
        P(),
        P(),
    )
    out_specs = (P("walk"), P("col", "walk"))
    run = functools.partial(body, mesh.shape["walk"], mesh.shape["col"])
    return jax.shard_map(run, mesh=mesh, in_specs=in_specs, out_specs=out_specs, check_vma=False)
```

```python
import functools
import math

import jax
import jax.numpy as jnp
from jax import lax
from jax.experimental import pallas as pl
from jax.experimental.pallas import tpu as pltpu
from jax.sharding import PartitionSpec as P

NROT = 16


momentum = 0.9
damping = 0.1


MESH = pl.DeviceIdType.MESH
PAD = 8
CHUNKS = 2


def icosa_points():
    golden = (1.0 + math.sqrt(5.0)) / 2.0
    length = math.sqrt(1.0 + golden * golden)
    rows = []
    for first in (-1.0, 1.0):
        for second in (-golden, golden):
            rows.append((0.0, first / length, second / length))
            rows.append((first / length, second / length, 0.0))
            rows.append((second / length, 0.0, first / length))
    return rows


def rotation_table(count):
    points = icosa_points()
    quad = len(points)
    angle = lax.broadcasted_iota(jnp.int32, (1, count), 1).astype(jnp.float32)
    turn_z = 2.0 * math.pi * angle / count
    turn_x = 0.9 * angle
    cz, sz = (jnp.cos(turn_z), jnp.sin(turn_z))
    cx, sx = (jnp.cos(turn_x), jnp.sin(turn_x))
    matrix = [[cz, -sz * cx, sz * sx], [sz, cz * cx, -cz * sx], [jnp.zeros_like(cz), sx, cx]]
    index = lax.broadcasted_iota(jnp.int32, (quad, count), 0)
    place = []
    for d in range(3):
        column = jnp.zeros((quad, count), jnp.float32)
        for j in range(quad):
            column = jnp.where(index == j, points[j][d], column)
        place.append(column)
    return [
        matrix[c][0] * place[0] + matrix[c][1] * place[1] + matrix[c][2] * place[2]
        for c in range(3)
    ]


def as_column(row):
    count = row.shape[1]
    index = lax.broadcasted_iota(jnp.int32, (count, count), 0)
    other = lax.broadcasted_iota(jnp.int32, (count, count), 1)
    return jnp.sum(jnp.where(index == other, row, 0.0), axis=1, keepdims=True)


def walker_energies(elec, atom, quad, rotation, channels, coef, expo, base, out):
    rows, points, atoms, electrons = quad.shape
    lmax = coef.shape[0]
    table = rotation_table(NROT)
    spot = [as_column(atom[c : c + 1, :]) for c in range(3)]
    count = as_column(channels[...].astype(jnp.float32))
    strength = [as_column(coef[level : level + 1, :]) for level in range(lmax)]
    decay = [as_column(expo[level : level + 1, :]) for level in range(lmax)]
    first = as_column(base[...])
    out[...] = jnp.zeros_like(out)
    kind = lax.broadcasted_iota(jnp.int32, (NROT, electrons), 0)

    def walker(w, _):
        onehot = (kind == rotation[pl.ds(w, 1), :]).astype(jnp.float32)
        turned = [
            jnp.dot(
                table[c], onehot, precision=lax.Precision.HIGHEST, preferred_element_type=jnp.float32
            )
            for c in range(3)
        ]
        where = elec[w]
        diff = [where[c : c + 1, :] - spot[c] for c in range(3)]
        dist2 = diff[0] * diff[0] + diff[1] * diff[1] + diff[2] * diff[2]
        root = jnp.sqrt(dist2 + 0.01)
        unit = [d / root for d in diff]
        angular = [jnp.zeros((atoms, electrons), jnp.float32) for _ in range(lmax)]
        for j in range(points):
            ratio = quad[w, j]
            cosang = unit[0] * turned[0][j : j + 1, :]
            cosang = cosang + unit[1] * turned[1][j : j + 1, :]
            cosang = cosang + unit[2] * turned[2][j : j + 1, :]
            lower, upper = None, None
            for level in range(lmax):
                if level == 0:
                    angular[0] = angular[0] + ratio
                    continue
                if level == 1:
                    lower, upper = 1.0, cosang
                else:
                    fresh = ((2 * level - 1) * cosang * upper - (level - 1) * lower) * (1.0 / level)
                    lower, upper = upper, fresh
                angular[level] = angular[level] + upper * ratio
        total = jnp.zeros((atoms, electrons), jnp.float32)
        for level in range(lmax):
            active = (count > level).astype(jnp.float32)
            radial = (strength[level] * active) * jnp.exp(-decay[level] * dist2)
            total = total + ((2 * level + 1) / points) * radial * angular[level]
        value = jnp.sum(jnp.sum(total, axis=1, keepdims=True), axis=0, keepdims=True)
        out[pl.ds(w, 1), :] = jnp.broadcast_to(value, (1, out.shape[1]))
        return 0

    lax.fori_loop(0, rows, walker, 0)
    out[0:rows, :] = out[0:rows, :] + first


def far_first(n):
    order, span = [], n
    while span > 1:
        order += [s for s in range(span // 2, n, span)]
        span //= 2
    return order + [s for s in range(1, n) if s not in order]


def step_kernel(
    n,
    m,
    finish,
    jac_ref,
    prev_ref,
    base_ref,
    elec_ref,
    atom_ref,
    quad_ref,
    rotation_ref,
    channels_ref,
    coef_ref,
    expo_ref,
    energy_ref,
    result_ref,
    cent_ref,
    prev,
    base,
    elec,
    atom,
    quad,
    rotation,
    channels,
    coef,
    expo,
    cols,
    part,
    shares,
    pair,
    full,
    energies,
    fetch_sem,
    jac_send,
    jac_recv,
    rs_send,
    rs_recv,
    pair_send,
    pair_recv,
    ag_send,
    ag_recv,
):
    me = lax.axis_index("walk")
    my_col = lax.axis_index("col")
    chunks, _, rows, span = cols.shape
    width = chunks * span
    walkers = rows * n
    scale = 1.0 / (width * n * m)
    order = far_first(n)
    barrier = pltpu.get_barrier_semaphore()
    for s in order:
        pl.semaphore_signal(
            barrier, inc=1, device_id=(lax.rem(me + s, n), my_col), device_id_type=MESH
        )
    for s in range(1, m):
        pl.semaphore_signal(
            barrier, inc=1, device_id=(me, lax.rem(my_col + s, m)), device_id_type=MESH
        )
    sources = (
        quad_ref,
        prev_ref,
        base_ref,
        elec_ref,
        atom_ref,
        rotation_ref,
        channels_ref,
        coef_ref,
        expo_ref,
    )
    targets = (quad, prev, base, elec, atom, rotation, channels, coef, expo)
    fetches = [
        pltpu.make_async_copy(source, target, fetch_sem.at[k])
        for k, (source, target) in enumerate(zip(sources, targets))
    ]
    for fetch in fetches:
        fetch.start()
    pl.semaphore_wait(barrier, n + m - 2)

    def block(index, k):
        return jac_ref.at[:, pl.ds(pl.multiple_of(index * width + k * span, span), span)]

    def send(src, dst, send_sem, recv_sem, s):
        pltpu.make_async_remote_copy(
            src_ref=src,
            dst_ref=dst.at[me],
            send_sem=send_sem,
            recv_sem=recv_sem,
            device_id=(lax.rem(me + s, n), my_col),
            device_id_type=MESH,
        ).start()

    def wait_bytes(like, sem):
        pltpu.make_async_copy(like, like, sem).wait()

    for k in range(chunks):
        for s in order:
            send(block(lax.rem(me + s, n), k), cols.at[k], jac_send.at[k], jac_recv.at[k], s)
        pltpu.make_async_copy(block(me, k), cols.at[k, me], jac_recv.at[k]).start()

    for fetch in fetches:
        fetch.wait()
    walker_energies(elec, atom, quad, rotation, channels, coef, expo, base, energies)
    cent_ref[...] = jnp.zeros_like(cent_ref)
    cent_ref[0, rows : rows + 1, :] = prev[...]

    gram = None
    for k in range(chunks):
        wait_bytes(cols.at[k], jac_recv.at[k])
        total = cols[k, 0]
        for i in range(1, n):
            total = total + cols[k, i]
        mean = jnp.sum(total, axis=0, keepdims=True) * (1.0 / walkers)
        for i in range(n):
            cent_ref[i, 0:rows, k * span : (k + 1) * span] = cols[k, i] - mean
        cent = cent_ref[:, :, k * span : (k + 1) * span].reshape(n * PAD, span)
        piece = lax.dot_general(
            cent,
            cent,
            (((1,), (1,)), ((), ())),
            precision=lax.Precision.HIGHEST,
            preferred_element_type=jnp.float32,
        )
        gram = piece if gram is None else gram + piece
    part[...] = gram.reshape(part.shape)

    for s in order:
        send(part.at[lax.rem(me + s, n)], shares, rs_send, rs_recv, s)
    shares[me] = part[me]
    wait_bytes(shares.at[pl.ds(0, n - 1)], rs_recv)
    acc = shares[0]
    for i in range(1, n):
        acc = acc + shares[i]
    pair[my_col] = acc

    def pair_copy(s, origin):
        return pltpu.make_async_remote_copy(
            src_ref=pair.at[my_col],
            dst_ref=pair.at[origin],
            send_sem=pair_send.at[s],
            recv_sem=pair_recv.at[origin],
            device_id=(me, lax.rem(my_col + s, m)),
            device_id_type=MESH,
        )

    for s in range(1, m):
        pair_copy(s, my_col).start()
    for s in range(1, m):
        pair_copy(s, lax.rem(my_col + s, m)).wait_recv()
    acc = pair[0]
    for c in range(1, m):
        acc = acc + pair[c]
    lane = lax.broadcasted_iota(jnp.int32, acc.shape, 1)
    spare = jnp.broadcast_to(energies[:, 0:1], acc.shape)
    full[me] = jnp.where(lane == rows + 1, spare, acc * scale)

    for s in order:
        send(full.at[me], full, ag_send, ag_recv, s)
    wait_bytes(full.at[pl.ds(0, n - 1)], ag_recv)
    if finish:
        solve(n, rows, full, cent_ref, prev, energies, result_ref, energy_ref)
    else:
        result_ref[...] = full[...]
        energy_ref[...] = jnp.broadcast_to(energies[0:rows, 0:1], (rows, 128))

    for k in range(chunks):
        wait_bytes(cols.at[k, pl.ds(0, n - 1)], jac_send.at[k])
    wait_bytes(part.at[pl.ds(0, n - 1)], rs_send)
    wait_bytes(full.at[pl.ds(0, n - 1)], ag_send)
    for s in range(1, m):
        pair_copy(s, my_col).wait_send()


def solve(n, rows, gram_ref, cent_ref, prev_ref, energy_ref, out_ref, mine_ref):
    index = lax.broadcasted_iota(jnp.int32, (rows, rows), 0)
    other = lax.broadcasted_iota(jnp.int32, (rows, rows), 1)
    mine_ref[...] = jnp.sum(
        jnp.where(index == other, energy_ref[0:rows, 0:rows], 0.0), axis=0, keepdims=True
    )
    wide = n * PAD
    walkers = n * rows
    sub = lax.broadcasted_iota(jnp.int32, (PAD, wide), 0)
    lane = lax.broadcasted_iota(jnp.int32, (PAD, wide), 1)
    real_row = sub < rows
    real = real_row & (lane % PAD < rows)
    energies = [
        jnp.broadcast_to(gram_ref[i][:, rows + 1 : rows + 2], (PAD, wide)) for i in range(n)
    ]
    esum = energies[0]
    for i in range(1, n):
        esum = esum + energies[i]
    emean = jnp.sum(jnp.where(real_row, esum, 0.0), axis=0, keepdims=True) * (1.0 / walkers)
    panels = []
    for i in range(n):
        g = gram_ref[i]
        eps = -(energies[i] - emean) * (1.0 / math.sqrt(walkers))
        along = jnp.broadcast_to(g[:, rows : rows + 1], (PAD, wide))
        right = eps - momentum * along
        panel = jnp.where(real, g, 0.0)
        panel = jnp.where(real & (lane == sub + i * PAD), panel + damping, panel)
        panels.append(jnp.where(real_row & (lane == rows), right, panel))

    def spread(panel, column):
        return jnp.broadcast_to(panel[:, column : column + 1], (PAD, wide))

    for g in range(n):
        top = panels[g]
        marks = [spread(top, g * PAD + r) for r in range(rows)]
        for r in range(rows):
            inverse = 1.0 / marks[r][r : r + 1, :]
            here = sub == r
            factor = jnp.where(here, 0.0, marks[r])
            line = top[r : r + 1, :] * inverse
            top = jnp.where(here, line, top - factor * line)
            for q in range(r + 1, rows):
                line_q = marks[q][r : r + 1, :] * inverse
                marks[q] = jnp.where(here, line_q, marks[q] - factor * line_q)
        for i in range(n):
            if i == g:
                continue
            panel = panels[i]
            fresh = panel
            for r in range(rows):
                fresh = fresh - spread(panel, g * PAD + r) * top[r : r + 1, :]
            panels[i] = fresh
        panels[g] = top

    width = cent_ref.shape[2]
    acc = jnp.zeros((PAD, width), jnp.float32)
    keep = lax.broadcasted_iota(jnp.int32, (PAD, width), 0) < rows
    for i in range(n):
        solved = jnp.broadcast_to(panels[i][:, rows : rows + 1], (PAD, width))
        acc = acc + solved * cent_ref[i]
    acc = jnp.where(keep, acc, 0.0)
    out_ref[...] = jnp.sum(acc, axis=0, keepdims=True) + momentum * prev_ref[...]


def step(n, m, jacobian, prev_update, base, elec_pos, atom_pos, quad, rotation, channels, coef, expo):
    rows = jacobian.shape[0]
    width = jacobian.shape[1] // n
    wide = n * PAD
    vmem = pl.BlockSpec(memory_space=pltpu.VMEM)
    hbm = pl.BlockSpec(memory_space=pltpu.HBM)
    f32 = jnp.float32
    dma = pltpu.SemaphoreType.DMA
    small = (prev_update, base, elec_pos, atom_pos, quad, rotation, channels, coef, expo)
    finish = wide <= 128
    gram = (n, PAD, wide)
    cent = (n, PAD, width)
    scratch = [pltpu.VMEM(x.shape, x.dtype) for x in small]
    if finish:
        shapes = [(1, rows), prev_update.shape]
        scratch = [pltpu.VMEM(cent, f32)] + scratch
    else:
        shapes = [(rows, 128), gram, cent]
    return pl.pallas_call(
        functools.partial(step_kernel, n, m, finish),
        out_shape=[jax.ShapeDtypeStruct(shape, f32) for shape in shapes],
        in_specs=[hbm] * 10,
        out_specs=[vmem] * len(shapes),
        scratch_shapes=scratch
        + [
            pltpu.VMEM((CHUNKS, n, rows, width // CHUNKS), f32),
            pltpu.VMEM(gram, f32),
            pltpu.VMEM(gram, f32),
            pltpu.VMEM((m, PAD, wide), f32),
            pltpu.VMEM(gram, f32),
            pltpu.VMEM((PAD, 128), f32),
        ]
        + [dma((len(small),)), dma((CHUNKS,)), dma((CHUNKS,)), dma, dma]
        + [dma((m,))] * 2
        + [dma] * 2,
        compiler_params=pltpu.CompilerParams(collective_id=0, has_side_effects=True, vmem_limit_bytes=60 * 1024 * 1024),
    )(jacobian, *small)


def hand_over_kernel(energy_in, result_in, energy_out, result_out):
    energy_out[...] = energy_in[...]
    result_out[...] = result_in[...]


def hand_over(energy, result):
    return pl.pallas_call(
        hand_over_kernel,
        out_shape=[jax.ShapeDtypeStruct(x.shape, x.dtype) for x in (energy, result)],
        compiler_params=pltpu.CompilerParams(vmem_limit_bytes=60 * 1024 * 1024),
    )(energy, result)


def finish_outside(n, rows, gram, cent, prev_update):
    walkers = n * rows
    along = gram[:, :rows, rows].reshape(walkers)
    energies = gram[:, :rows, rows + 1].reshape(walkers)
    square = gram.reshape(n, PAD, n, PAD)[:, :rows, :, :rows].reshape(walkers, walkers)
    eps = -(energies - jnp.mean(energies)) / math.sqrt(walkers)
    system = square + damping * jnp.eye(walkers, dtype=jnp.float32)
    factor = jnp.linalg.cholesky(system)
    solved = jax.scipy.linalg.cho_solve((factor, True), eps - momentum * along)
    flat = cent[:, :rows, :].reshape(walkers, -1)
    update = jnp.dot(
        solved, flat, precision=lax.Precision.HIGHEST, preferred_element_type=jnp.float32
    )
    return update[None, :] + momentum * prev_update


def body(
    n,
    m,
    jacobian,
    prev_update,
    base_energy,
    elec_pos,
    atom_pos,
    quad_ratio,
    rotation,
    channels,
    ecp_coef,
    ecp_expo,
):
    rows = jacobian.shape[0]
    energy, result, *cent = step(
        n,
        m,
        jacobian,
        prev_update,
        base_energy.reshape(1, -1),
        elec_pos,
        atom_pos,
        jnp.transpose(quad_ratio, (0, 3, 1, 2)),
        rotation,
        channels.reshape(1, -1),
        ecp_coef.T,
        ecp_expo.T,
    )
    if cent:
        return (energy[:, 0], finish_outside(n, rows, result, cent[0], prev_update))
    energy, result = hand_over(energy, result)
    return (energy.reshape(rows), result)


def solution(mesh):
    in_specs = (
        P("walk", "col"),
        P("col", "walk"),
        P("walk"),
        P("walk", None, None),
        P(),
        P("walk", None, None, None),
        P("walk", None),
        P(),
        P(),
        P(),
    )
    out_specs = (P("walk"), P("col", "walk"))
    run = functools.partial(body, mesh.shape["walk"], mesh.shape["col"])
    return jax.shard_map(run, mesh=mesh, in_specs=in_specs, out_specs=out_specs, check_vma=False)
```
